32 devices in a mesh: edp: 4 (over x, core), ep: 8 (over z, y).
Axes of the slice: x: 2, y: 2, z: 4, core: 2. Of those that a mesh axis runs over, the one named last changes fastest.
Arguments:
- tokens: bfloat16 [4096, 5120], P(('edp', 'ep')), may hold values from -6 to 6
- cotangent: bfloat16 [4096, 5120], P(('edp', 'ep')), may hold values from -4 to 4
- gate_probs: bfloat16 [4096, 6], P(('edp', 'ep')), may hold values from 0.099609375 to 1
- expert_ids: int32 [4096, 6], P(('edp', 'ep')), may hold values from 0 to 159, all different within a row
- w_gate: bfloat16 [8, 1536, 5120], P('ep', 'edp'), may hold values from -0.078125 to 0.078125
- w_up: bfloat16 [8, 1536, 5120], P('ep', 'edp'), may hold values from -0.078125 to 0.078125
- w_down: bfloat16 [8, 1536, 5120], P('ep', 'edp'), may hold values from -0.15625 to 0.15625
Outputs:
- token_grad: bfloat16 [4096, 5120], P(('edp', 'ep'))
- gate_grad: bfloat16 [4096, 6], P(('edp', 'ep'))
- gate_wgrad: bfloat16 [8, 1536, 5120], P('ep', 'edp')
- up_wgrad: bfloat16 [8, 1536, 5120], P('ep', 'edp')
- down_wgrad: bfloat16 [8, 1536, 5120], P('ep', 'edp')
The draws below stay inside these ranges and needn't reach their ends.
Inputs may be any that keep to these rules, and one draw needn't show every extreme that they name: `expert_ids`: each row holds 6 different ids, and every id appears in some row.
All inputs are finite; a program needn't handle non-finite values.
Results may differ from the reference program's by a relative error of at most 0.008.
Values may be sent and summed in bfloat16 or wider, within the bound.
A program may use at most 128 MiB of HBM per device.

```python
import math
import jax
import jax.numpy as jnp
from jax import lax

D = 5120
H = 1536
ALL_EXPERTS = 160
TOP = 6
EXP_EP = 1
TOK_DEV = 128
EXPERTS = 8
SPLIT = 4
CAP = 3
TOKENS = 4096
N_EDP = 4
N_EP = 8


def block_levels(rng, extent, cuts, smallest, largest):
    gain = 1.0
    for position, shards_of in cuts:
        steps = jax.random.uniform(jax.random.fold_in(jax.random.fold_in(rng, 6), position), (shards_of,), jnp.float32, smallest / len(cuts), largest / len(cuts))
        gain = gain * jnp.repeat(jnp.exp(steps), extent[position] // shards_of).reshape((-1,) + (1,) * (len(extent) - 1 - position))
    return gain


def picks_of(key, rows, count, top, lift):
    ranking = jax.random.permutation(jax.random.fold_in(key, 1), count)
    pull = ranking
    for power in range(3):
        pull = pull * pull // count
    pull = pull * lift // count
    chance = jax.random.randint(jax.random.fold_in(key, 2), (rows, count), 0, 4096) + pull
    sure = jax.random.permutation(jax.random.fold_in(key, 3), rows)[jnp.arange(count) % rows]
    chance = jnp.where(jnp.arange(rows)[:, None] == sure[None, :], 1 << 14, chance)
    merit = chance * count + jnp.arange(count)
    return lax.top_k(merit.astype(jnp.int32), top)[1].astype(jnp.int32)


def centred(rng, shape, width, most, shards=(), kind=jnp.bfloat16):
    level = block_levels(rng, shape, shards, -0.22, 0.18) if shards else 1.0
    array = jax.random.normal(rng, shape, jnp.float32) * width * level
    return jnp.minimum(jnp.maximum(array, -most), most).astype(kind)


def setup_inputs(seed: int = 0) -> dict:
    key_list = jax.random.split(jax.random.key(seed), 8)
    return {
        "tokens": centred(key_list[0], (TOKENS, D), 1.0, 6.0, ((0, 32),)),
        "cotangent": centred(key_list[1], (TOKENS, D), 0.5, 4.0, ((0, 32),)),
        "gate_probs": jnp.clip(jnp.exp(math.log(1.0) - 2.306499 * jax.random.uniform(key_list[2], (TOKENS, TOP), jnp.float32) ** block_levels(key_list[2], (TOKENS, TOP), ((0, 32),), -0.2, 0.2)), 0.099609375, 1.0).astype(jnp.bfloat16),
        "expert_ids": picks_of(key_list[3], TOKENS, ALL_EXPERTS, TOP, 614),
        "w_gate": centred(key_list[4], (N_EP, EXP_EP * H, D), D ** -0.5, 0.078125, ((0, 8), (1, 4))),
        "w_up": centred(key_list[5], (N_EP, EXP_EP * H, D), D ** -0.5, 0.078125, ((0, 8), (1, 4))),
        "w_down": centred(key_list[6], (N_EP, EXP_EP * H, D), H ** -0.5, 0.15625, ((0, 8), (1, 4))),
    }


def route_tables(expert_ids, experts, capacity):
    tok_count = expert_ids.shape[0]
    matches = (expert_ids[:, :, None] == jnp.arange(experts, dtype=jnp.int32)[None, None, :]).astype(jnp.float32)
    counts = jnp.sum(matches, axis=1)
    positions = jnp.arange(tok_count, dtype=jnp.int32)
    earlier = (positions[None, :] < positions[:, None]).astype(jnp.float32)
    before = jnp.dot(earlier, counts, precision=lax.Precision.HIGHEST)
    slot_pos = jnp.sum(matches * before[:, None, :], axis=2)
    column = expert_ids.astype(jnp.float32) * capacity + slot_pos
    inside = (expert_ids < experts) & (slot_pos < capacity)
    targets = jnp.arange(experts * capacity, dtype=jnp.float32)
    hits = inside[:, :, None] & (column[:, :, None] == targets[None, None, :])
    return jnp.where(hits, 1.0, 0.0).astype(jnp.float32)


def expert_step(operands):
    rows_x, rows_dy, rows_p, gate_mat, up_mat, down_mat = operands
    contract = (((1,), (1,)), ((), ()))
    pre_gate = lax.dot_general(rows_x, gate_mat, contract, preferred_element_type=jnp.float32)
    pre_up = lax.dot_general(rows_x, up_mat, contract, preferred_element_type=jnp.float32)
    sigma_gate = jax.nn.sigmoid(pre_gate)
    hidden = pre_gate * sigma_gate * pre_up
    back_hid = lax.dot_general(rows_dy, down_mat, contract, preferred_element_type=jnp.float32)
    slot_dp = jnp.sum(hidden * back_hid, axis=1)
    prob_col = rows_p.astype(jnp.float32)[:, None]
    grad_hid = prob_col * back_hid
    grad_gate = (grad_hid * pre_up * sigma_gate * (1.0 + pre_gate * (1.0 - sigma_gate))).astype(jnp.bfloat16)
    grad_up = (grad_hid * pre_gate * sigma_gate).astype(jnp.bfloat16)
    scaled_cot = (prob_col * rows_dy.astype(jnp.float32)).astype(jnp.bfloat16)
    hidden_half = hidden.astype(jnp.bfloat16)
    outer = (((0,), (0,)), ((), ()))
    down_grad = lax.dot_general(hidden_half, scaled_cot, outer, preferred_element_type=jnp.float32).astype(jnp.bfloat16)
    gate_grad = lax.dot_general(grad_gate, rows_x, outer, preferred_element_type=jnp.float32).astype(jnp.bfloat16)
    up_grad = lax.dot_general(grad_up, rows_x, outer, preferred_element_type=jnp.float32).astype(jnp.bfloat16)
    slice_width = H // SPLIT
    row_total = rows_x.shape[0]
    gate_slices = grad_gate.reshape(row_total, SPLIT, slice_width).transpose(1, 0, 2)
    up_slices = grad_up.reshape(row_total, SPLIT, slice_width).transpose(1, 0, 2)
    gate_blocks = gate_mat.reshape(SPLIT, slice_width, D)
    up_blocks = up_mat.reshape(SPLIT, slice_width, D)

    def add_slice(running, pieces):
        left_gate, left_up, right_gate, right_up = pieces
        partial_sum = jnp.dot(left_gate, right_gate, preferred_element_type=jnp.float32)
        partial_sum = partial_sum + jnp.dot(left_up, right_up, preferred_element_type=jnp.float32)
        rounded = lax.optimization_barrier(partial_sum.astype(jnp.bfloat16))
        return running + rounded.astype(jnp.float32), None

    start_sum = jnp.zeros((row_total, D), jnp.float32)
    slot_dx, unused = lax.scan(add_slice, start_sum, (gate_slices, up_slices, gate_blocks, up_blocks))
    return slot_dx.astype(jnp.bfloat16), slot_dp.astype(jnp.bfloat16), gate_grad, up_grad, down_grad


def reference(tokens, cotangent, gate_probs, expert_ids, w_gate, w_up, w_down):
    blocks = N_EDP * N_EP
    experts = EXPERTS
    tok_blocks = tokens.reshape(blocks, TOK_DEV, D)
    cot_blocks = cotangent.reshape(blocks, TOK_DEV, D)
    prob_blocks = gate_probs.reshape(blocks, TOK_DEV, TOP).astype(jnp.float32)
    id_blocks = expert_ids.reshape(blocks, TOK_DEV, TOP)
    tables = jax.vmap(lambda ids: route_tables(ids, experts, CAP))(id_blocks)
    route_matrix = jnp.sum(tables, axis=2)
    sent_x = jnp.einsum('btc,btd->bcd', route_matrix, tok_blocks.astype(jnp.float32)).astype(jnp.bfloat16)
    sent_dy = jnp.einsum('btc,btd->bcd', route_matrix, cot_blocks.astype(jnp.float32)).astype(jnp.bfloat16)
    sent_p = jnp.einsum('btrc,btr->bc', tables, prob_blocks).astype(jnp.bfloat16)
    rows_x = sent_x.reshape(blocks, experts, CAP, D).transpose(1, 0, 2, 3).reshape(experts, blocks * CAP, D)
    rows_dy = sent_dy.reshape(blocks, experts, CAP, D).transpose(1, 0, 2, 3).reshape(experts, blocks * CAP, D)
    rows_p = sent_p.reshape(blocks, experts, CAP).transpose(1, 0, 2).reshape(experts, blocks * CAP)
    gate_all = w_gate.reshape(experts, H, D)
    up_all = w_up.reshape(experts, H, D)
    down_all = w_down.reshape(experts, H, D)
    slot_dx, slot_gp, gate_wgrad, up_wgrad, down_wgrad = lax.map(
        expert_step, (rows_x, rows_dy, rows_p, gate_all, up_all, down_all))
    back_x = slot_dx.reshape(experts, blocks, CAP, D).transpose(1, 0, 2, 3).reshape(blocks, experts * CAP, D)
    back_p = slot_gp.reshape(experts, blocks, CAP).transpose(1, 0, 2).reshape(blocks, experts * CAP)
    token_grad = jnp.einsum('btc,bcd->btd', route_matrix, back_x.astype(jnp.float32)).astype(jnp.bfloat16)
    gate_grad = jnp.einsum('btrc,bc->btr', tables, back_p.astype(jnp.float32)).astype(jnp.bfloat16)
    shape_out = (N_EP, EXP_EP * H, D)
    return (token_grad.reshape(TOKENS, D), gate_grad.reshape(TOKENS, TOP),
            gate_wgrad.reshape(shape_out), up_wgrad.reshape(shape_out), down_wgrad.reshape(shape_out))
```

```python
import functools

import jax
import jax.numpy as jnp
import numpy as np
from jax import lax
from jax.experimental import pallas as pl
from jax.experimental.pallas import tpu as pltpu
from jax.sharding import PartitionSpec as P

CAP = 3
SUB = 8
LANES = 128
WIDE = SUB * LANES
MESH = pl.DeviceIdType.MESH
F32 = jnp.float32
BF16 = jnp.bfloat16
NT = (((1,), (1,)), ((), ()))
TN = (((0,), (0,)), ((), ()))


def order_matrix(n_ep, per):
    unit = CAP * per
    rows = n_ep * SUB * unit
    out = np.zeros((rows, rows), np.float32)
    for e in range(n_ep):
        for k in range(SUB):
            for kind in range(per):
                for s in range(CAP):
                    out[
                        (e * SUB + k) * unit + kind * CAP + s,
                        ((k * per + kind) * n_ep + e) * CAP + s,
                    ] = 1.0
    return out


def routes(ids, probs, columns):
    tok = ids.shape[0]
    lane = lax.broadcasted_iota(jnp.int32, (tok, LANES), 1)
    expert = lane // CAP
    slot = lane - expert * CAP
    match = jnp.zeros((tok, LANES), F32)
    weight = jnp.zeros((tok, LANES), F32)
    for r in range(ids.shape[1]):
        here = (ids[:, r : r + 1] == expert) & (lane < columns)
        match = jnp.where(here, 1.0, match)
        weight = jnp.where(here, probs[:, r : r + 1].astype(F32), weight)
    row = lax.broadcasted_iota(jnp.int32, (tok, tok), 0)
    col = lax.broadcasted_iota(jnp.int32, (tok, tok), 1)
    earlier = jnp.where(col < row, 1.0, 0.0).astype(BF16)
    before = jnp.dot(earlier, match.astype(BF16), preferred_element_type=F32)
    live = jnp.where(before == slot.astype(F32), match, 0.0)
    return live, live * weight


def main_kernel(
    n_edp, n_ep,
    tok_ref, cot_ref, probs_ref, ids_ref, wg_ref, wu_ref, wd_ref, ord2_ref, ord2t_ref, ord1_ref, ord1t_ref,
    z_out, left_out, back_out, live_out, gp_out,
    w, send_a, recv_a, z, acc, send_b, recv_b, send_c, recv_c, own, send_d, recv_d,
    dp, dp_b, dp_s, dp_c, dp_own, dp_d, dp_r,
    w_sem, z_sem, loc_sem, a_ss, a_rs, e_ss, e_rs, f_ss, f_rs, b_ss, b_rs, c_ss, c_rs, d_ss, d_rs,
    pb_s, pc_ss, pc_rs, pd_ss, pd_rs,
):
    n_ch = z.shape[0]
    hid = wg_ref.shape[1]
    half = n_ep * CAP
    n_q = n_edp // 2
    me_i = lax.axis_index("edp")
    me_j = lax.axis_index("ep")
    q_me = me_i // 2
    core = me_i - q_me * 2
    mate = q_me * 2 + 1 - core

    def w_copy(c, part):
        src = (wg_ref, wu_ref, wd_ref)[part]
        return pltpu.make_async_copy(
            src.at[0, :, pl.ds(pl.multiple_of(c * WIDE, WIDE), WIDE)],
            w.at[c, pl.ds(part * hid, hid), :],
            w_sem.at[c, part],
        )

    barrier = pltpu.get_barrier_semaphore()
    ep_peers = [lax.rem(me_j + o, n_ep) for o in range(1, n_ep)]
    far = [(lax.rem(q_me + o, n_q), o) for o in range(1, n_q)]
    for j in ep_peers:
        pl.semaphore_signal(barrier, inc=1, device_id=(me_i, j), device_id_type=MESH)
    for q, _ in far:
        pl.semaphore_signal(barrier, inc=1, device_id=(q * 2 + core, me_j), device_id_type=MESH)
    pl.semaphore_signal(barrier, inc=1, device_id=(mate, me_j), device_id_type=MESH)

    live, scaled = routes(ids_ref[...], probs_ref[...], half)
    live_out[...] = live.astype(BF16)
    live_t = live.T[:half].astype(BF16)
    scaled_t = scaled.T[:half].astype(BF16)
    prob = jnp.sum(scaled, axis=0, keepdims=True)

    pl.semaphore_wait(barrier, n_ep - 1 + n_q - 1 + 1)

    def remote(src, dst, ss, rs, i, j):
        return pltpu.make_async_remote_copy(
            src_ref=src, dst_ref=dst, send_sem=ss, recv_sem=rs, device_id=(i, j), device_id_type=MESH
        )

    def a_copy(c, j, slot):
        return remote(send_a.at[c, j], recv_a.at[c, slot], a_ss.at[c, j], a_rs.at[c, slot], me_i, j)

    def a_own(c):
        return pltpu.make_async_copy(send_a.at[c, me_j], recv_a.at[c, me_j], loc_sem.at[c])

    def pack(c, _):
        cols = pl.ds(pl.multiple_of(c * WIDE, WIDE), WIDE)
        x = jnp.dot(live_t, tok_ref[:, cols], preferred_element_type=F32)
        y = jnp.dot(scaled_t, cot_ref[:, cols], preferred_element_type=F32)
        parts = []
        for k in range(SUB):
            lanes = slice(k * LANES, (k + 1) * LANES)
            parts += [x[:, lanes], y[:, lanes]]
        mixed = jnp.concatenate(parts, axis=0).astype(BF16)
        packed = jnp.dot(ord2_ref[...], mixed, preferred_element_type=F32)
        send_a[c] = packed.astype(BF16).reshape(send_a.shape[1:])
        for j in ep_peers:
            a_copy(c, j, me_j).start()
        a_own(c).start()
        for part in range(3):
            w_copy(c, part).start()
        return 0

    lax.fori_loop(0, n_ch, pack, 0)

    def e_copy(c, i, slot, o):
        return remote(z.at[c, me_i], z.at[c, slot], e_ss.at[c, o], e_rs.at[c, o], i, me_j)

    def f_copy(c, slot, o):
        return remote(z.at[c, slot], z.at[c, slot], f_ss.at[c, o], f_rs.at[c, o], mate, me_j)

    def gather(t, _):
        @pl.when(t < n_ch)
        def _():
            c = t
            for j in ep_peers:
                a_copy(c, j, j).wait_recv()
            a_own(c).wait()
            mixed = recv_a[c].reshape(ord2_ref.shape[0], LANES)
            rows = jnp.dot(ord2t_ref[...], mixed, preferred_element_type=F32)
            wide = jnp.concatenate(
                [rows[k * 2 * half : (k + 1) * 2 * half] for k in range(SUB)], axis=1
            )
            z[c, me_i] = wide.astype(BF16)
            for q, o in far:
                e_copy(c, q * 2 + core, me_i, o).start()
            e_copy(c, mate, me_i, 0).start()

        @pl.when((t >= 1) & (t < n_ch + 1))
        def _():
            c = t - 1
            for _, o in far:
                from_q = lax.rem(q_me - o + n_q, n_q)
                e_copy(c, from_q * 2 + core, from_q * 2 + core, o).wait_recv()
                f_copy(c, from_q * 2 + core, o).start()

        @pl.when(t >= 2)
        def _():
            c = t - 2
            e_copy(c, mate, mate, 0).wait_recv()
            for _, o in far:
                from_q = lax.rem(q_me - o + n_q, n_q)
                f_copy(c, from_q * 2 + 1 - core, o).wait_recv()
            for part in range(3):
                w_copy(c, part).wait()
            rows = z[c].reshape(n_edp * 2 * half, WIDE)
            part = lax.dot_general(rows, w[c], NT, preferred_element_type=F32)

            @pl.when(c == 0)
            def _():
                acc[...] = part

            @pl.when(c > 0)
            def _():
                acc[...] += part

        return 0

    lax.fori_loop(0, n_ch + 2, gather, 0)

    def z_copy(c):
        return pltpu.make_async_copy(z.at[c], z_out.at[c], z_sem.at[c])

    def z_start(c, _):
        z_copy(c).start()
        return 0

    lax.fori_loop(0, n_ch, z_start, 0)

    both = []
    left = []
    none = jnp.zeros((half, hid), F32)
    for i in range(n_edp):
        first = i * 2 * half
        a = acc[first : first + half, :hid]
        u = acc[first : first + half, hid : 2 * hid]
        g = acc[first + half : first + 2 * half, 2 * hid :]
        s = jax.nn.sigmoid(a)
        h = a * s * u
        d_a = g * u * s * (1.0 + a * (1.0 - s))
        d_u = g * a * s
        both.append(jnp.concatenate([d_a, d_u], axis=1))
        left.append(jnp.concatenate([d_a, d_u, none], axis=1))
        left.append(jnp.concatenate([none, none, h], axis=1))
        dp[i] = jnp.broadcast_to(jnp.sum(h * g, axis=1, keepdims=True), (half, LANES))
    both = jnp.concatenate(both, axis=0).astype(BF16)
    left_out[...] = jnp.concatenate(left, axis=0).astype(BF16)

    def b_copy(c, q):
        return remote(
            send_b.at[c, q * 2 + 1 - core], recv_b.at[c, q], b_ss.at[c, q], b_rs.at[c, q], mate, me_j
        )

    def dpb_copy(q):
        return remote(dp.at[q * 2 + 1 - core], dp_b.at[q], pb_s.at[0, q], pb_s.at[1, q], mate, me_j)

    def c_copy(c, q, o):
        return remote(
            send_c.at[c, o - 1], recv_c.at[c, o - 1], c_ss.at[c, o - 1], c_rs.at[c, o - 1], q * 2 + core, me_j
        )

    def dpc_copy(q, o):
        return remote(
            dp_s.at[o - 1], dp_c.at[o - 1], pc_ss.at[o - 1], pc_rs.at[o - 1], q * 2 + core, me_j
        )

    def d_copy(c, j, slot):
        return remote(send_d.at[c, j], recv_d.at[c, slot], d_ss.at[c, j], d_rs.at[c, slot], me_i, j)

    def dpd_copy(j, slot):
        return remote(dp_d, dp_r.at[slot], pd_ss.at[j], pd_rs.at[slot], me_i, j)

    for q in range(n_q):
        dpb_copy(q).start()

    def give_back(t, _):
        @pl.when(t < n_ch)
        def _():
            c = t
            part = jnp.dot(both, w[c, : 2 * hid, :], preferred_element_type=F32)
            for i in range(n_edp):
                send_b[c, i] = part[i * half : (i + 1) * half].astype(BF16)
            for q in range(n_q):
                b_copy(c, q).start()

        @pl.when((t >= 1) & (t < n_ch + 1))
        def _():
            c = t - 1
            for q in range(n_q):
                b_copy(c, q).wait_recv()
            for q, o in far:
                total = send_b[c, q * 2 + core].astype(F32) + recv_b[c, q].astype(F32)
                send_c[c, o - 1] = total.astype(BF16)
                c_copy(c, q, o).start()
            own[c] = send_b[c, me_i].astype(F32) + recv_b[c, q_me].astype(F32)

        @pl.when(t >= 2)
        def _():
            c = t - 2
            total = own[c]
            for q, o in far:
                c_copy(c, q, o).wait_recv()
                total = total + recv_c[c, o - 1].astype(F32)
            mixed = jnp.concatenate(
                [total[:, k * LANES : (k + 1) * LANES] for k in range(SUB)], axis=0
            ).astype(BF16)
            packed = jnp.dot(ord1_ref[...], mixed, preferred_element_type=F32)
            send_d[c] = packed.astype(BF16).reshape(send_d.shape[1:])
            for j in ep_peers:
                d_copy(c, j, me_j).start()
            recv_d[c, me_j] = send_d[c, me_j]

        return 0

    lax.fori_loop(0, n_ch + 2, give_back, 0)

    for q in range(n_q):
        dpb_copy(q).wait_recv()
    for q, o in far:
        dp_s[o - 1] = dp[q * 2 + core] + dp_b[q]
        dpc_copy(q, o).start()
    total = dp[me_i] + dp_b[q_me]
    for q, o in far:
        dpc_copy(q, o).wait_recv()
        total = total + dp_c[o - 1]
    square = jnp.concatenate([total, jnp.zeros((LANES - half, LANES), F32)], axis=0)
    dp_d[...] = square.T[:1]
    for j in ep_peers:
        dpd_copy(j, me_j).start()
    dp_r[me_j] = dp_d[...]

    def finish(c, _):
        for j in ep_peers:
            d_copy(c, j, j).wait_recv()
        mixed = recv_d[c].reshape(ord1_ref.shape[0], LANES)
        rows = jnp.dot(ord1t_ref[...], mixed, preferred_element_type=F32)
        wide = jnp.concatenate([rows[k * half : (k + 1) * half] for k in range(SUB)], axis=1)
        back_out[c] = wide.astype(BF16)
        return 0

    lax.fori_loop(0, n_ch, finish, 0)

    for j in ep_peers:
        dpd_copy(j, j).wait_recv()
    lane = lax.broadcasted_iota(jnp.int32, (1, LANES), 1)
    got = jnp.zeros((1, LANES), F32)
    for e in range(n_ep):
        for s in range(CAP):
            value = jnp.sum(
                jnp.where(lane == me_j * CAP + s, dp_r[e], 0.0), axis=1, keepdims=True
            )
            got = jnp.where(lane == e * CAP + s, value, got)
    gp_out[...] = jnp.where(prob > 0.0, got / jnp.where(prob > 0.0, prob, 1.0), 0.0)

    def drain(c, _):
        for j in ep_peers:
            a_copy(c, j, me_j).wait_send()
            d_copy(c, j, me_j).wait_send()
        e_copy(c, mate, me_i, 0).wait_send()
        for q, o in far:
            e_copy(c, q * 2 + core, me_i, o).wait_send()
            f_copy(c, q * 2 + core, o).wait_send()
            c_copy(c, q, o).wait_send()
        for q in range(n_q):
            b_copy(c, q).wait_send()
        z_copy(c).wait()
        return 0

    lax.fori_loop(0, n_ch, drain, 0)
    for q in range(n_q):
        dpb_copy(q).wait_send()
    for q, o in far:
        dpc_copy(q, o).wait_send()
    for j in ep_peers:
        dpd_copy(j, me_j).wait_send()


def exchange(n_edp, n_ep, tokens, cotangent, gate_probs, expert_ids, w_gate, w_up, w_down):
    tok, width = tokens.shape
    hid = w_gate.shape[1]
    half = n_ep * CAP
    n_q = n_edp // 2
    n_far = max(n_q - 1, 1)
    n_ch = width // WIDE
    two = order_matrix(n_ep, 2)
    one = order_matrix(n_ep, 1)
    orders = [jnp.asarray(m, BF16) for m in (two, two.T, one, one.T)]
    vmem = pl.BlockSpec(memory_space=pltpu.VMEM)
    hbm = pl.BlockSpec(memory_space=pl.ANY)
    dma = pltpu.SemaphoreType.DMA
    rows = n_edp * 2 * half
    return pl.pallas_call(
        functools.partial(main_kernel, n_edp, n_ep),
        out_shape=(
            jax.ShapeDtypeStruct((n_ch, n_edp, 2 * half, WIDE), BF16),
            jax.ShapeDtypeStruct((rows, 3 * hid), BF16),
            jax.ShapeDtypeStruct((n_ch, half, WIDE), BF16),
            jax.ShapeDtypeStruct((tok, LANES), BF16),
            jax.ShapeDtypeStruct((1, LANES), F32),
        ),
        in_specs=[vmem] * 4 + [hbm] * 3 + [vmem] * 4,
        out_specs=(hbm, vmem, vmem, vmem, vmem),
        scratch_shapes=[
            pltpu.VMEM((n_ch, 3 * hid, WIDE), BF16),
            pltpu.VMEM((n_ch, n_ep, SUB * 2 * CAP, LANES), BF16),
            pltpu.VMEM((n_ch, n_ep, SUB * 2 * CAP, LANES), BF16),
            pltpu.VMEM((n_ch, n_edp, 2 * half, WIDE), BF16),
            pltpu.VMEM((rows, 3 * hid), F32),
            pltpu.VMEM((n_ch, n_edp, half, WIDE), BF16),
            pltpu.VMEM((n_ch, n_q, half, WIDE), BF16),
            pltpu.VMEM((n_ch, n_far, half, WIDE), BF16),
            pltpu.VMEM((n_ch, n_far, half, WIDE), BF16),
            pltpu.VMEM((n_ch, half, WIDE), F32),
            pltpu.VMEM((n_ch, n_ep, SUB * CAP, LANES), BF16),
            pltpu.VMEM((n_ch, n_ep, SUB * CAP, LANES), BF16),
            pltpu.VMEM((n_edp, half, LANES), F32),
            pltpu.VMEM((n_q, half, LANES), F32),
            pltpu.VMEM((n_far, half, LANES), F32),
            pltpu.VMEM((n_far, half, LANES), F32),
            pltpu.VMEM((half, LANES), F32),
            pltpu.VMEM((1, LANES), F32),
            pltpu.VMEM((n_ep, 1, LANES), F32),
            dma((n_ch, 3)),
            dma((n_ch,)),
            dma((n_ch,)),
            dma((n_ch, n_ep)),
            dma((n_ch, n_ep)),
            dma((n_ch, n_q)),
            dma((n_ch, n_q)),
            dma((n_ch, n_q)),
            dma((n_ch, n_q)),
            dma((n_ch, n_q)),
            dma((n_ch, n_q)),
            dma((n_ch, n_far)),
            dma((n_ch, n_far)),
            dma((n_ch, n_ep)),
            dma((n_ch, n_ep)),
            dma((2, n_q)),
            dma((n_far,)),
            dma((n_far,)),
            dma((n_ep,)),
            dma((n_ep,)),
        ],
        compiler_params=pltpu.CompilerParams(
            collective_id=0, has_side_effects=True, vmem_limit_bytes=60 * 2**20
        ),
    )(tokens, cotangent, gate_probs, expert_ids, w_gate, w_up, w_down, *orders)


def grads_kernel(half, z_ref, left_ref, back_ref, live_ref, gp_ref, ids_ref, tg_ref, gg_ref, wg_ref, wu_ref, wd_ref):
    hid = wg_ref.shape[1]
    rows = z_ref[0].reshape(left_ref.shape[0], WIDE)
    for part, out in enumerate((wg_ref, wu_ref, wd_ref)):
        out[0] = lax.dot_general(
            left_ref[:, part * hid : (part + 1) * hid], rows, TN, preferred_element_type=F32
        ).astype(BF16)
    live = live_ref[...]
    tg_ref[...] = jnp.dot(live[:, :half], back_ref[0], preferred_element_type=F32).astype(BF16)

    @pl.when(pl.program_id(0) == 0)
    def _():
        ids = ids_ref[...]
        expert = lax.broadcasted_iota(jnp.int32, live.shape, 1) // CAP
        value = live.astype(F32) * gp_ref[...]
        for r in range(ids.shape[1]):
            mine = jnp.where(ids[:, r : r + 1] == expert, value, 0.0)
            gg_ref[:, r : r + 1] = jnp.sum(mine, axis=1, keepdims=True).astype(BF16)


def per_device(tokens, cotangent, gate_probs, expert_ids, w_gate, w_up, w_down):
    n_edp = lax.axis_size("edp")
    n_ep = lax.axis_size("ep")
    half = n_ep * CAP
    z, left, back, live, gp = exchange(
        n_edp, n_ep, tokens, cotangent, gate_probs, expert_ids, w_gate, w_up, w_down
    )
    n_ch = z.shape[0]
    tok, width = tokens.shape
    hid = w_gate.shape[1]
    rows = left.shape[0]

    def whole(shape):
        return pl.BlockSpec(shape, lambda c: (0,) * len(shape))

    w_spec = pl.BlockSpec((1, hid, WIDE), lambda c: (0, 0, c))
    w_shape = jax.ShapeDtypeStruct(w_gate.shape, BF16)
    return pl.pallas_call(
        functools.partial(grads_kernel, half),
        grid=(n_ch,),
        out_shape=(
            jax.ShapeDtypeStruct((tok, width), BF16),
            jax.ShapeDtypeStruct(gate_probs.shape, BF16),
            w_shape,
            w_shape,
            w_shape,
        ),
        in_specs=[
            pl.BlockSpec((1, n_edp, 2 * half, WIDE), lambda c: (c, 0, 0, 0)),
            whole((rows, 3 * hid)),
            pl.BlockSpec((1, half, WIDE), lambda c: (c, 0, 0)),
            whole((tok, LANES)),
            whole((1, LANES)),
            whole(expert_ids.shape),
        ],
        out_specs=(
            pl.BlockSpec((tok, WIDE), lambda c: (0, c)),
            whole(gate_probs.shape),
            w_spec,
            w_spec,
            w_spec,
        ),
        compiler_params=pltpu.CompilerParams(vmem_limit_bytes=48 * 2**20),
    )(z, left, back, live, gp, expert_ids)


def solution(mesh):
    rows = P(("edp", "ep"), None)
    weights = P("ep", "edp", None)
    return jax.shard_map(
        per_device,
        mesh=mesh,
        in_specs=(rows, rows, rows, rows, weights, weights, weights),
        out_specs=(rows, rows, weights, weights, weights),
        check_vma=False,
    )
```

```python
import functools

import jax
import jax.numpy as jnp
import numpy as np
from jax import lax
from jax.experimental import pallas as pl
from jax.experimental.pallas import tpu as pltpu
from jax.sharding import PartitionSpec as P

CAP = 3
SUB = 8
LANES = 128
WIDE = SUB * LANES
MESH = pl.DeviceIdType.MESH
F32 = jnp.float32
BF16 = jnp.bfloat16
NT = (((1,), (1,)), ((), ()))
TN = (((0,), (0,)), ((), ()))


def order_matrix(n_ep, per):
    unit = CAP * per
    rows = n_ep * SUB * unit
    out = np.zeros((rows, rows), np.float32)
    for e in range(n_ep):
        for k in range(SUB):
            for kind in range(per):
                for s in range(CAP):
                    out[
                        (e * SUB + k) * unit + kind * CAP + s,
                        ((k * per + kind) * n_ep + e) * CAP + s,
                    ] = 1.0
    return out


def routes(ids, probs, columns):
    tok = ids.shape[1]
    row = lax.broadcasted_iota(jnp.int32, (columns, tok), 0)
    expert = row // CAP
    slot = row - expert * CAP
    match = jnp.zeros((columns, tok), F32)
    weight = jnp.zeros((columns, tok), F32)
    for r in range(ids.shape[0]):
        here = ids[r : r + 1] == expert
        match = jnp.where(here, 1.0, match)
        weight = jnp.where(here, probs[r : r + 1], weight)
    first = lax.broadcasted_iota(jnp.int32, (tok, tok), 0)
    second = lax.broadcasted_iota(jnp.int32, (tok, tok), 1)
    earlier = jnp.where(first < second, 1.0, 0.0).astype(BF16)
    before = jnp.dot(match.astype(BF16), earlier, preferred_element_type=F32)
    live = jnp.where(before == slot.astype(F32), match, 0.0)
    return live, live * weight


def main_kernel(
    n_edp, n_ep,
    tok_ref, cot_ref, probs_ref, ids_ref, wg_ref, wu_ref, wd_ref, ord2_ref, ord2t_ref, ord1_ref, ord1t_ref,
    z_out, left_out, back_out, live_out, gp_out,
    tok, cot, w, send_a, recv_a, z, acc, send_b, recv_b, send_c, recv_c, own, send_d, recv_d,
    dp, dp_b, dp_s, dp_c, dp_d, dp_r,
    t_sem, w_sem, z_sem, loc_sem, a_ss, a_rs, e_ss, e_rs, f_ss, f_rs, b_ss, b_rs, c_ss, c_rs, d_ss, d_rs,
    pb_s, pc_ss, pc_rs, pd_ss, pd_rs,
):
    n_ch = z.shape[0]
    hid = wg_ref.shape[1]
    half = n_ep * CAP
    n_q = n_edp // 2
    me_i = lax.axis_index("edp")
    me_j = lax.axis_index("ep")
    q_me = me_i // 2
    core = me_i - q_me * 2
    mate = q_me * 2 + 1 - core

    def w_copy(c, part):
        src = (wg_ref, wu_ref, wd_ref)[part]
        return pltpu.make_async_copy(
            src.at[0, :, pl.ds(pl.multiple_of(c * WIDE, WIDE), WIDE)],
            w.at[c, pl.ds(part * hid, hid), :],
            w_sem.at[c, part],
        )

    def t_copy(c, part):
        src, dst = ((tok_ref, tok), (cot_ref, cot))[part]
        return pltpu.make_async_copy(
            src.at[:, pl.ds(pl.multiple_of(c * WIDE, WIDE), WIDE)], dst.at[c], t_sem.at[c, part]
        )

    for c in range(n_ch):
        t_copy(c, 0).start()
        t_copy(c, 1).start()

    barrier = pltpu.get_barrier_semaphore()
    ep_peers = [lax.rem(me_j + o, n_ep) for o in range(1, n_ep)]
    far = [(lax.rem(q_me + o, n_q), o) for o in range(1, n_q)]
    for j in ep_peers:
        pl.semaphore_signal(barrier, inc=1, device_id=(me_i, j), device_id_type=MESH)
    for q, _ in far:
        pl.semaphore_signal(barrier, inc=1, device_id=(q * 2 + core, me_j), device_id_type=MESH)
    pl.semaphore_signal(barrier, inc=1, device_id=(mate, me_j), device_id_type=MESH)

    live, scaled = routes(ids_ref[...], probs_ref[...], half)
    live_out[...] = live.astype(BF16)
    live_t = live.astype(BF16)
    scaled_t = scaled.astype(BF16)
    prob = jnp.sum(scaled, axis=1, keepdims=True)

    pl.semaphore_wait(barrier, n_ep - 1 + n_q - 1 + 1)

    def remote(src, dst, ss, rs, i, j):
        return pltpu.make_async_remote_copy(
            src_ref=src, dst_ref=dst, send_sem=ss, recv_sem=rs, device_id=(i, j), device_id_type=MESH
        )

    def a_copy(c, j, slot):
        return remote(send_a.at[c, j], recv_a.at[c, slot], a_ss.at[c, j], a_rs.at[c, slot], me_i, j)

    def a_own(c):
        return pltpu.make_async_copy(send_a.at[c, me_j], recv_a.at[c, me_j], loc_sem.at[c])

    def pack(c, _):
        t_copy(c, 0).wait()
        t_copy(c, 1).wait()
        x = jnp.dot(live_t, tok[c], preferred_element_type=F32)
        y = jnp.dot(scaled_t, cot[c], preferred_element_type=F32)
        parts = []
        for k in range(SUB):
            lanes = slice(k * LANES, (k + 1) * LANES)
            parts += [x[:, lanes], y[:, lanes]]
        mixed = jnp.concatenate(parts, axis=0).astype(BF16)
        packed = jnp.dot(ord2_ref[...], mixed, preferred_element_type=F32)
        send_a[c] = packed.astype(BF16).reshape(send_a.shape[1:])
        for j in ep_peers:
            a_copy(c, j, me_j).start()
        a_own(c).start()
        for part in range(3):
            w_copy(c, part).start()
        return 0

    lax.fori_loop(0, n_ch, pack, 0)

    def e_copy(c, i, slot, o):
        return remote(z.at[c, me_i], z.at[c, slot], e_ss.at[c, o], e_rs.at[c, o], i, me_j)

    def f_copy(c, slot, o):
        return remote(z.at[c, slot], z.at[c, slot], f_ss.at[c, o], f_rs.at[c, o], mate, me_j)

    def gather(t, _):
        @pl.when(t < n_ch)
        def _():
            c = t
            for j in ep_peers:
                a_copy(c, j, j).wait_recv()
            a_own(c).wait()
            mixed = recv_a[c].reshape(ord2_ref.shape[0], LANES)
            rows = jnp.dot(ord2t_ref[...], mixed, preferred_element_type=F32)
            wide = jnp.concatenate(
                [rows[k * 2 * half : (k + 1) * 2 * half] for k in range(SUB)], axis=1
            )
            z[c, me_i] = wide.astype(BF16)
            for q, o in far:
                e_copy(c, q * 2 + core, me_i, o).start()
            e_copy(c, mate, me_i, 0).start()

        @pl.when((t >= 1) & (t < n_ch + 1))
        def _():
            c = t - 1
            for _, o in far:
                from_q = lax.rem(q_me - o + n_q, n_q)
                e_copy(c, from_q * 2 + core, from_q * 2 + core, o).wait_recv()
                f_copy(c, from_q * 2 + core, o).start()

        @pl.when(t >= 2)
        def _():
            c = t - 2
            e_copy(c, mate, mate, 0).wait_recv()
            for _, o in far:
                from_q = lax.rem(q_me - o + n_q, n_q)
                f_copy(c, from_q * 2 + 1 - core, o).wait_recv()
            for part in range(3):
                w_copy(c, part).wait()
            rows = z[c].reshape(n_edp * 2 * half, WIDE)
            part = lax.dot_general(w[c], rows, NT, preferred_element_type=F32)

            @pl.when(c == 0)
            def _():
                acc[...] = part

            @pl.when(c > 0)
            def _():
                acc[...] += part

        return 0

    lax.fori_loop(0, n_ch + 2, gather, 0)

    def z_copy(c):
        return pltpu.make_async_copy(z.at[c], z_out.at[c], z_sem.at[c])

    def z_start(c, _):
        z_copy(c).start()
        return 0

    lax.fori_loop(0, n_ch, z_start, 0)

    n_rows = n_edp * 2 * half
    a = acc[:hid]
    u = acc[hid : 2 * hid]
    g = pltpu.roll(acc[2 * hid :], n_rows - half, 1)
    lane = lax.broadcasted_iota(jnp.int32, (hid, n_rows), 1)
    is_x = lax.rem(lane // half, 2) == 0
    s = jax.nn.sigmoid(a)
    h = a * s * u
    d_a = jnp.where(is_x, g * u * s * (1.0 + a * (1.0 - s)), 0.0)
    d_u = jnp.where(is_x, g * a * s, 0.0)
    acc[:hid] = d_a
    acc[hid : 2 * hid] = d_u
    acc[2 * hid :] = jnp.where(is_x, h, 0.0)
    dp[...] = jnp.sum(jnp.where(is_x, h * g, 0.0), axis=0, keepdims=True)
    both = acc[: 2 * hid].T.astype(BF16)

    def b_copy(c, q):
        return remote(
            send_b.at[c, q * 2 + 1 - core], recv_b.at[c, q], b_ss.at[c, q], b_rs.at[c, q], mate, me_j
        )

    def dpb_copy():
        return remote(dp, dp_b, pb_s.at[0], pb_s.at[1], mate, me_j)

    def c_copy(c, q, o):
        return remote(
            send_c.at[c, o - 1], recv_c.at[c, o - 1], c_ss.at[c, o - 1], c_rs.at[c, o - 1], q * 2 + core, me_j
        )

    def dpc_copy(q, o):
        return remote(dp_s, dp_c.at[o - 1], pc_ss.at[o - 1], pc_rs.at[o - 1], q * 2 + core, me_j)

    def d_copy(c, j, slot):
        return remote(send_d.at[c, j], recv_d.at[c, slot], d_ss.at[c, j], d_rs.at[c, slot], me_i, j)

    def dpd_copy(j, slot):
        return remote(dp_d, dp_r.at[slot], pd_ss.at[j], pd_rs.at[slot], me_i, j)

    dpb_copy().start()

    def give_back(t, _):
        @pl.when(t < n_ch)
        def _():
            c = t
            part = jnp.dot(both, w[c, : 2 * hid, :], preferred_element_type=F32)
            for i in range(n_edp):
                send_b[c, i] = part[i * 2 * half : (i * 2 + 1) * half].astype(BF16)
            for q in range(n_q):
                b_copy(c, q).start()

        @pl.when((t >= 1) & (t < n_ch + 1))
        def _():
            c = t - 1
            for q in range(n_q):
                b_copy(c, q).wait_recv()
            for q, o in far:
                total = send_b[c, q * 2 + core].astype(F32) + recv_b[c, q].astype(F32)
                send_c[c, o - 1] = total.astype(BF16)
                c_copy(c, q, o).start()
            own[c] = send_b[c, me_i].astype(F32) + recv_b[c, q_me].astype(F32)

            @pl.when(c == 0)
            def _():
                dpb_copy().wait_recv()
                dp_s[...] = dp[...] + dp_b[...]
                for q, o in far:
                    dpc_copy(q, o).start()

        @pl.when(t >= 2)
        def _():
            c = t - 2
            total = own[c]
            for q, o in far:
                c_copy(c, q, o).wait_recv()
                total = total + recv_c[c, o - 1].astype(F32)
            mixed = jnp.concatenate(
                [total[:, k * LANES : (k + 1) * LANES] for k in range(SUB)], axis=0
            ).astype(BF16)
            packed = jnp.dot(ord1_ref[...], mixed, preferred_element_type=F32)
            send_d[c] = packed.astype(BF16).reshape(send_d.shape[1:])
            for j in ep_peers:
                d_copy(c, j, me_j).start()
            recv_d[c, me_j] = send_d[c, me_j]

            @pl.when(c == 0)
            def _():
                whole_dp = dp_s[...]
                for q, o in far:
                    dpc_copy(q, o).wait_recv()
                    whole_dp = whole_dp + dp_c[o - 1]
                dp_d[...] = whole_dp
                dp_r[me_j] = whole_dp
                for j in ep_peers:
                    dpd_copy(j, me_j).start()

        return 0

    lax.fori_loop(0, n_ch + 2, give_back, 0)

    spin = pltpu.roll(acc[2 * hid :], half, 1)
    left_out[: 2 * hid] = acc[: 2 * hid].astype(BF16)
    left_out[2 * hid :] = spin.astype(BF16)

    def finish(c, _):
        for j in ep_peers:
            d_copy(c, j, j).wait_recv()
        mixed = recv_d[c].reshape(ord1_ref.shape[0], LANES)
        rows = jnp.dot(ord1t_ref[...], mixed, preferred_element_type=F32)
        wide = jnp.concatenate([rows[k * half : (k + 1) * half] for k in range(SUB)], axis=1)
        back_out[c] = wide.astype(BF16)
        return 0

    lax.fori_loop(0, n_ch, finish, 0)

    for j in ep_peers:
        dpd_copy(j, j).wait_recv()
    at = lax.broadcasted_iota(jnp.int32, (1, n_rows), 1) - (me_i * 2 * half + me_j * CAP)
    row = lax.broadcasted_iota(jnp.int32, (half, 1), 0)
    got = jnp.zeros((half, 1), F32)
    for e in range(n_ep):
        for slot in range(CAP):
            value = jnp.sum(jnp.where(at == slot, dp_r[e], 0.0), axis=1, keepdims=True)
            got = jnp.where(row == e * CAP + slot, value, got)
    got = jnp.where(prob > 0.0, got / jnp.where(prob > 0.0, prob, 1.0), 0.0)
    gp_out[...] = jnp.broadcast_to(got, gp_out.shape)

    def drain(c, _):
        for j in ep_peers:
            a_copy(c, j, me_j).wait_send()
            d_copy(c, j, me_j).wait_send()
        e_copy(c, mate, me_i, 0).wait_send()
        for q, o in far:
            e_copy(c, q * 2 + core, me_i, o).wait_send()
            f_copy(c, q * 2 + core, o).wait_send()
            c_copy(c, q, o).wait_send()
        for q in range(n_q):
            b_copy(c, q).wait_send()
        z_copy(c).wait()
        return 0

    lax.fori_loop(0, n_ch, drain, 0)
    dpb_copy().wait_send()
    for q, o in far:
        dpc_copy(q, o).wait_send()
    for j in ep_peers:
        dpd_copy(j, me_j).wait_send()


def exchange(n_edp, n_ep, tokens, cotangent, gate_probs, expert_ids, w_gate, w_up, w_down):
    tok, width = tokens.shape
    hid = w_gate.shape[1]
    half = n_ep * CAP
    n_q = n_edp // 2
    n_far = max(n_q - 1, 1)
    n_ch = width // WIDE
    two = order_matrix(n_ep, 2)
    one = order_matrix(n_ep, 1)
    orders = [jnp.asarray(m, BF16) for m in (two, two.T, one, one.T)]
    vmem = pl.BlockSpec(memory_space=pltpu.VMEM)
    hbm = pl.BlockSpec(memory_space=pl.ANY)
    dma = pltpu.SemaphoreType.DMA
    rows = n_edp * 2 * half
    return pl.pallas_call(
        functools.partial(main_kernel, n_edp, n_ep),
        out_shape=(
            jax.ShapeDtypeStruct((n_ch, n_edp, 2 * half, WIDE), BF16),
            jax.ShapeDtypeStruct((3 * hid, rows), BF16),
            jax.ShapeDtypeStruct((n_ch, half, WIDE), BF16),
            jax.ShapeDtypeStruct((half, tok), BF16),
            jax.ShapeDtypeStruct((half, tok), F32),
        ),
        in_specs=[hbm] * 2 + [vmem] * 2 + [hbm] * 3 + [vmem] * 4,
        out_specs=(hbm, vmem, vmem, vmem, vmem),
        scratch_shapes=[
            pltpu.VMEM((n_ch, tok, WIDE), BF16),
            pltpu.VMEM((n_ch, tok, WIDE), BF16),
            pltpu.VMEM((n_ch, 3 * hid, WIDE), BF16),
            pltpu.VMEM((n_ch, n_ep, SUB * 2 * CAP, LANES), BF16),
            pltpu.VMEM((n_ch, n_ep, SUB * 2 * CAP, LANES), BF16),
            pltpu.VMEM((n_ch, n_edp, 2 * half, WIDE), BF16),
            pltpu.VMEM((3 * hid, rows), F32),
            pltpu.VMEM((n_ch, n_edp, half, WIDE), BF16),
            pltpu.VMEM((n_ch, n_q, half, WIDE), BF16),
            pltpu.VMEM((n_ch, n_far, half, WIDE), BF16),
            pltpu.VMEM((n_ch, n_far, half, WIDE), BF16),
            pltpu.VMEM((n_ch, half, WIDE), F32),
            pltpu.VMEM((n_ch, n_ep, SUB * CAP, LANES), BF16),
            pltpu.VMEM((n_ch, n_ep, SUB * CAP, LANES), BF16),
            pltpu.VMEM((1, rows), F32),
            pltpu.VMEM((1, rows), F32),
            pltpu.VMEM((1, rows), F32),
            pltpu.VMEM((n_far, 1, rows), F32),
            pltpu.VMEM((1, rows), F32),
            pltpu.VMEM((n_ep, 1, rows), F32),
            dma((n_ch, 2)),
            dma((n_ch, 3)),
            dma((n_ch,)),
            dma((n_ch,)),
            dma((n_ch, n_ep)),
            dma((n_ch, n_ep)),
            dma((n_ch, n_q)),
            dma((n_ch, n_q)),
            dma((n_ch, n_q)),
            dma((n_ch, n_q)),
            dma((n_ch, n_q)),
            dma((n_ch, n_q)),
            dma((n_ch, n_far)),
            dma((n_ch, n_far)),
            dma((n_ch, n_ep)),
            dma((n_ch, n_ep)),
            dma((2,)),
            dma((n_far,)),
            dma((n_far,)),
            dma((n_ep,)),
            dma((n_ep,)),
        ],
        compiler_params=pltpu.CompilerParams(
            collective_id=0, has_side_effects=True, vmem_limit_bytes=60 * 2**20
        ),
    )(tokens, cotangent, gate_probs.T.astype(F32), expert_ids.T, w_gate, w_up, w_down, *orders)


def grads_kernel(z_ref, left_ref, back_ref, live_ref, gp_ref, ids_ref, tg_ref, gg_ref, wg_ref, wu_ref, wd_ref):
    hid = wg_ref.shape[1]
    rows = z_ref[0].reshape(left_ref.shape[1], WIDE)
    for part, out in enumerate((wg_ref, wu_ref, wd_ref)):
        out[0] = jnp.dot(
            left_ref[part * hid : (part + 1) * hid], rows, preferred_element_type=F32
        ).astype(BF16)
    live = live_ref[...]
    tg_ref[...] = lax.dot_general(live, back_ref[0], TN, preferred_element_type=F32).astype(BF16)

    @pl.when(pl.program_id(0) == 0)
    def _():
        ids = ids_ref[...]
        expert = lax.broadcasted_iota(jnp.int32, live.shape, 0) // CAP
        value = live.astype(F32) * gp_ref[...]
        for r in range(ids.shape[0]):
            mine = jnp.where(ids[r : r + 1] == expert, value, 0.0)
            gg_ref[r : r + 1] = jnp.sum(mine, axis=0, keepdims=True)


def per_device(tokens, cotangent, gate_probs, expert_ids, w_gate, w_up, w_down):
    n_edp = lax.axis_size("edp")
    n_ep = lax.axis_size("ep")
    half = n_ep * CAP
    z, left, back, live, gp = exchange(
        n_edp, n_ep, tokens, cotangent, gate_probs, expert_ids, w_gate, w_up, w_down
    )
    n_ch = z.shape[0]
    tok, width = tokens.shape
    hid = w_gate.shape[1]
    rows = left.shape[1]
    top = gate_probs.shape[1]

    def whole(shape):
        return pl.BlockSpec(shape, lambda c: (0,) * len(shape))

    w_spec = pl.BlockSpec((1, hid, WIDE), lambda c: (0, 0, c))
    w_shape = jax.ShapeDtypeStruct(w_gate.shape, BF16)
    token_grad, gate_grad, *weight_grads = pl.pallas_call(
        grads_kernel,
        grid=(n_ch,),
        out_shape=(
            jax.ShapeDtypeStruct((tok, width), BF16),
            jax.ShapeDtypeStruct((top, tok), F32),
            w_shape,
            w_shape,
            w_shape,
        ),
        in_specs=[
            pl.BlockSpec((1, n_edp, 2 * half, WIDE), lambda c: (c, 0, 0, 0)),
            whole((3 * hid, rows)),
            pl.BlockSpec((1, half, WIDE), lambda c: (c, 0, 0)),
            whole((half, tok)),
            whole((half, tok)),
            whole((top, tok)),
        ],
        out_specs=(
            pl.BlockSpec((tok, WIDE), lambda c: (0, c)),
            whole((top, tok)),
            w_spec,
            w_spec,
            w_spec,
        ),
        compiler_params=pltpu.CompilerParams(vmem_limit_bytes=63 * 2**20),
    )(z, left, back, live, gp, expert_ids.T)
    return (token_grad, gate_grad.T.astype(BF16), *weight_grads)


def solution(mesh):
    rows = P(("edp", "ep"), None)
    weights = P("ep", "edp", None)
    return jax.shard_map(
        per_device,
        mesh=mesh,
        in_specs=(rows, rows, rows, rows, weights, weights, weights),
        out_specs=(rows, rows, weights, weights, weights),
        check_vma=False,
    )
```

```python
import functools

import jax
import jax.numpy as jnp
import numpy as np
from jax import lax
from jax.experimental import pallas as pl
from jax.experimental.pallas import tpu as pltpu
from jax.sharding import PartitionSpec as P

CAP = 3
LEAD = 2
SUB = 8
LANES = 128
WIDE = SUB * LANES
MESH = pl.DeviceIdType.MESH
F32 = jnp.float32
BF16 = jnp.bfloat16
NT = (((1,), (1,)), ((), ()))
TN = (((0,), (0,)), ((), ()))


def order_matrix(n_ep, per):
    unit = CAP * per
    rows = n_ep * SUB * unit
    out = np.zeros((rows, rows), np.float32)
    for e in range(n_ep):
        for k in range(SUB):
            for kind in range(per):
                for s in range(CAP):
                    out[
                        (e * SUB + k) * unit + kind * CAP + s,
                        ((k * per + kind) * n_ep + e) * CAP + s,
                    ] = 1.0
    return out


def routes(ids, probs, columns):
    tok = ids.shape[1]
    row = lax.broadcasted_iota(jnp.int32, (columns, tok), 0)
    expert = row // CAP
    slot = row - expert * CAP
    match = jnp.zeros((columns, tok), F32)
    weight = jnp.zeros((columns, tok), F32)
    for r in range(ids.shape[0]):
        here = ids[r : r + 1] == expert
        match = jnp.where(here, 1.0, match)
        weight = jnp.where(here, probs[r : r + 1], weight)
    first = lax.broadcasted_iota(jnp.int32, (tok, tok), 0)
    second = lax.broadcasted_iota(jnp.int32, (tok, tok), 1)
    earlier = jnp.where(first < second, 1.0, 0.0).astype(BF16)
    before = jnp.dot(match.astype(BF16), earlier, preferred_element_type=F32)
    live = jnp.where(before == slot.astype(F32), match, 0.0)
    return live, live * weight


def main_kernel(
    n_edp, n_ep,
    tok_ref, cot_ref, probs_ref, ids_ref, wg_ref, wu_ref, wd_ref, ord2_ref, ord2t_ref, ord1_ref, ord1t_ref,
    z_out, gate_out, up_out, down_out, back_out, live_out, gg_out,
    tok, cot, w, send_a, recv_a, z, acc, send_b, recv_b, send_c, recv_c, own, send_d, recv_d,
    dp, dp_b, dp_s, dp_c, dp_d, dp_r,
    t_sem, w_sem, z_sem, loc_sem, a_ss, a_rs, e_ss, e_rs, f_ss, f_rs, b_ss, b_rs, c_ss, c_rs, d_ss, d_rs,
    pb_s, pc_ss, pc_rs, pd_ss, pd_rs,
):
    n_ch = z.shape[0]
    hid = wg_ref.shape[1]
    half = n_ep * CAP
    n_q = n_edp // 2
    me_i = lax.axis_index("edp")
    me_j = lax.axis_index("ep")
    q_me = me_i // 2
    core = me_i - q_me * 2
    mate = q_me * 2 + 1 - core

    def w_copy(c, part):
        src = (wg_ref, wu_ref, wd_ref)[part]
        return pltpu.make_async_copy(
            src.at[0, :, pl.ds(pl.multiple_of(c * WIDE, WIDE), WIDE)],
            w.at[c, pl.ds(part * hid, hid), :],
            w_sem.at[c, part],
        )

    def t_copy(c, part):
        src, dst = ((tok_ref, tok), (cot_ref, cot))[part]
        return pltpu.make_async_copy(
            src.at[:, pl.ds(pl.multiple_of(c * WIDE, WIDE), WIDE)], dst.at[c], t_sem.at[c, part]
        )

    for c in range(n_ch):
        t_copy(c, 0).start()
        t_copy(c, 1).start()

    barrier = pltpu.get_barrier_semaphore()
    ep_peers = [lax.rem(me_j + o, n_ep) for o in range(1, n_ep)]
    far = [(lax.rem(q_me + o, n_q), o) for o in range(1, n_q)]
    for j in ep_peers:
        pl.semaphore_signal(barrier, inc=1, device_id=(me_i, j), device_id_type=MESH)
    for q, _ in far:
        pl.semaphore_signal(barrier, inc=1, device_id=(q * 2 + core, me_j), device_id_type=MESH)
    pl.semaphore_signal(barrier, inc=1, device_id=(mate, me_j), device_id_type=MESH)

    live, scaled = routes(ids_ref[...], probs_ref[...].astype(F32), half)
    live_out[...] = live.astype(BF16)
    live_t = live.astype(BF16)
    scaled_t = scaled.astype(BF16)
    prob = jnp.sum(scaled, axis=1, keepdims=True)

    pl.semaphore_wait(barrier, n_ep - 1 + n_q - 1 + 1)

    def remote(src, dst, ss, rs, i, j):
        return pltpu.make_async_remote_copy(
            src_ref=src, dst_ref=dst, send_sem=ss, recv_sem=rs, device_id=(i, j), device_id_type=MESH
        )

    def a_copy(c, j, slot):
        return remote(send_a.at[c, j], recv_a.at[c, slot], a_ss.at[c, j], a_rs.at[c, slot], me_i, j)

    def a_own(c):
        return pltpu.make_async_copy(send_a.at[c, me_j], recv_a.at[c, me_j], loc_sem.at[c])

    def pack(c):
        t_copy(c, 0).wait()
        t_copy(c, 1).wait()
        x = jnp.dot(live_t, tok[c], preferred_element_type=F32)
        y = jnp.dot(scaled_t, cot[c], preferred_element_type=F32)
        parts = []
        for k in range(SUB):
            lanes = slice(k * LANES, (k + 1) * LANES)
            parts += [x[:, lanes], y[:, lanes]]
        mixed = jnp.concatenate(parts, axis=0).astype(BF16)
        packed = jnp.dot(ord2_ref[...], mixed, preferred_element_type=F32)
        send_a[c] = packed.astype(BF16).reshape(send_a.shape[1:])
        for j in ep_peers:
            a_copy(c, j, me_j).start()
        a_own(c).start()
        for part in range(3):
            w_copy(c, part).start()


    def e_copy(c, i, slot, o):
        return remote(z.at[c, me_i], z.at[c, slot], e_ss.at[c, o], e_rs.at[c, o], i, me_j)

    def f_copy(c, slot, o):
        return remote(z.at[c, slot], z.at[c, slot], f_ss.at[c, o], f_rs.at[c, o], mate, me_j)

    def gather(t, _):
        @pl.when(t < n_ch)
        def _():
            pack(t)

        @pl.when((t >= LEAD) & (t < n_ch + LEAD))
        def _():
            c = t - LEAD
            for j in ep_peers:
                a_copy(c, j, j).wait_recv()
            a_own(c).wait()
            mixed = recv_a[c].reshape(ord2_ref.shape[0], LANES)
            rows = jnp.dot(ord2t_ref[...], mixed, preferred_element_type=F32)
            wide = jnp.concatenate(
                [rows[k * 2 * half : (k + 1) * 2 * half] for k in range(SUB)], axis=1
            )
            z[c, me_i] = wide.astype(BF16)
            for q, o in far:
                e_copy(c, q * 2 + core, me_i, o).start()
            e_copy(c, mate, me_i, 0).start()

        @pl.when((t >= LEAD + 1) & (t < n_ch + LEAD + 1))
        def _():
            c = t - LEAD - 1
            for _, o in far:
                from_q = lax.rem(q_me - o + n_q, n_q)
                e_copy(c, from_q * 2 + core, from_q * 2 + core, o).wait_recv()
                f_copy(c, from_q * 2 + core, o).start()

        @pl.when(t >= LEAD + 2)
        def _():
            c = t - LEAD - 2
            e_copy(c, mate, mate, 0).wait_recv()
            for _, o in far:
                from_q = lax.rem(q_me - o + n_q, n_q)
                f_copy(c, from_q * 2 + 1 - core, o).wait_recv()
            for part in range(3):
                w_copy(c, part).wait()
            rows = z[c].reshape(n_edp * 2 * half, WIDE)
            part = lax.dot_general(w[c], rows, NT, preferred_element_type=F32)

            @pl.when(c == 0)
            def _():
                acc[...] = part

            @pl.when(c > 0)
            def _():
                acc[...] += part

        return 0

    lax.fori_loop(0, n_ch + LEAD + 2, gather, 0)

    def z_copy(c):
        return pltpu.make_async_copy(
            z.at[c], z_out.at[:, :, pl.ds(pl.multiple_of(c * WIDE, WIDE), WIDE)], z_sem.at[c]
        )

    def z_start(c, _):
        z_copy(c).start()
        return 0

    lax.fori_loop(0, n_ch, z_start, 0)

    n_rows = n_edp * 2 * half
    a = acc[:hid]
    u = acc[hid : 2 * hid]
    g = pltpu.roll(acc[2 * hid :], n_rows - half, 1)
    lane = lax.broadcasted_iota(jnp.int32, (hid, n_rows), 1)
    is_x = lax.rem(lane // half, 2) == 0
    s = jax.nn.sigmoid(a)
    h = a * s * u
    d_a = jnp.where(is_x, g * u * s * (1.0 + a * (1.0 - s)), 0.0)
    d_u = jnp.where(is_x, g * a * s, 0.0)
    acc[:hid] = d_a
    acc[hid : 2 * hid] = d_u
    acc[2 * hid :] = jnp.where(is_x, h, 0.0)
    dp[...] = jnp.sum(jnp.where(is_x, h * g, 0.0), axis=0, keepdims=True)
    turned = acc[: 2 * hid].T
    both = jnp.concatenate(
        [turned[i * 2 * half : (i * 2 + 1) * half] for i in range(n_edp)], axis=0
    ).astype(BF16)

    def b_copy(c, q):
        return remote(
            send_b.at[c, q * 2 + 1 - core], recv_b.at[c, q], b_ss.at[c, q], b_rs.at[c, q], mate, me_j
        )

    def dpb_copy():
        return remote(dp, dp_b, pb_s.at[0], pb_s.at[1], mate, me_j)

    def c_copy(c, q, o):
        return remote(
            send_c.at[c, o - 1], recv_c.at[c, o - 1], c_ss.at[c, o - 1], c_rs.at[c, o - 1], q * 2 + core, me_j
        )

    def dpc_copy(q, o):
        return remote(dp_s, dp_c.at[o - 1], pc_ss.at[o - 1], pc_rs.at[o - 1], q * 2 + core, me_j)

    def d_copy(c, j, slot):
        return remote(send_d.at[c, j], recv_d.at[c, slot], d_ss.at[c, j], d_rs.at[c, slot], me_i, j)

    def dpd_copy(j, slot):
        return remote(dp_d, dp_r.at[slot], pd_ss.at[j], pd_rs.at[slot], me_i, j)

    dpb_copy().start()

    def give_back(t, _):
        @pl.when(t < n_ch)
        def _():
            c = t
            part = jnp.dot(both, w[c, : 2 * hid, :], preferred_element_type=F32)
            for i in range(n_edp):
                send_b[c, i] = part[i * half : (i + 1) * half].astype(BF16)
            for q in range(n_q):
                b_copy(c, q).start()

        @pl.when((t >= 1) & (t < n_ch + 1))
        def _():
            c = t - 1
            for q in range(n_q):
                b_copy(c, q).wait_recv()
            for q, o in far:
                total = send_b[c, q * 2 + core].astype(F32) + recv_b[c, q].astype(F32)
                send_c[c, o - 1] = total.astype(BF16)
                c_copy(c, q, o).start()
            own[c] = send_b[c, me_i].astype(F32) + recv_b[c, q_me].astype(F32)

            @pl.when(c == 0)
            def _():
                dpb_copy().wait_recv()
                dp_s[...] = dp[...] + dp_b[...]
                for q, o in far:
                    dpc_copy(q, o).start()

        @pl.when(t >= 2)
        def _():
            c = t - 2
            total = own[c]
            for q, o in far:
                c_copy(c, q, o).wait_recv()
                total = total + recv_c[c, o - 1].astype(F32)
            mixed = jnp.concatenate(
                [total[:, k * LANES : (k + 1) * LANES] for k in range(SUB)], axis=0
            ).astype(BF16)
            packed = jnp.dot(ord1_ref[...], mixed, preferred_element_type=F32)
            send_d[c] = packed.astype(BF16).reshape(send_d.shape[1:])
            for j in ep_peers:
                d_copy(c, j, me_j).start()
            recv_d[c, me_j] = send_d[c, me_j]

            @pl.when(c == 0)
            def _():
                whole_dp = dp_s[...]
                for q, o in far:
                    dpc_copy(q, o).wait_recv()
                    whole_dp = whole_dp + dp_c[o - 1]
                dp_d[...] = whole_dp
                dp_r[me_j] = whole_dp
                for j in ep_peers:
                    dpd_copy(j, me_j).start()

        return 0

    lax.fori_loop(0, n_ch + 2, give_back, 0)

    spin = pltpu.roll(acc[2 * hid :], half, 1)
    gate_out[...] = acc[:hid].astype(BF16)
    up_out[...] = acc[hid : 2 * hid].astype(BF16)
    down_out[...] = spin.astype(BF16)

    def finish(c, _):
        for j in ep_peers:
            d_copy(c, j, j).wait_recv()
        mixed = recv_d[c].reshape(ord1_ref.shape[0], LANES)
        rows = jnp.dot(ord1t_ref[...], mixed, preferred_element_type=F32)
        wide = jnp.concatenate([rows[k * half : (k + 1) * half] for k in range(SUB)], axis=1)
        back_out[:, pl.ds(pl.multiple_of(c * WIDE, WIDE), WIDE)] = wide.astype(BF16)
        return 0

    lax.fori_loop(0, n_ch, finish, 0)

    for j in ep_peers:
        dpd_copy(j, j).wait_recv()
    at = lax.broadcasted_iota(jnp.int32, (1, n_rows), 1) - (me_i * 2 * half + me_j * CAP)
    row = lax.broadcasted_iota(jnp.int32, (half, 1), 0)
    got = jnp.zeros((half, 1), F32)
    for e in range(n_ep):
        for slot in range(CAP):
            value = jnp.sum(jnp.where(at == slot, dp_r[e], 0.0), axis=1, keepdims=True)
            got = jnp.where(row == e * CAP + slot, value, got)
    got = jnp.where(prob > 0.0, got / jnp.where(prob > 0.0, prob, 1.0), 0.0)
    got = got.astype(BF16).astype(F32)
    value = live * got
    owner = lax.broadcasted_iota(jnp.int32, live.shape, 0) // CAP
    grads = []
    for r in range(ids_ref.shape[0]):
        mine = jnp.where(ids_ref[r : r + 1] == owner, value, 0.0)
        grads.append(jnp.sum(mine, axis=0, keepdims=True))
    gg_out[...] = jnp.concatenate(grads, axis=0).astype(BF16)

    def drain(c, _):
        for j in ep_peers:
            a_copy(c, j, me_j).wait_send()
            d_copy(c, j, me_j).wait_send()
        e_copy(c, mate, me_i, 0).wait_send()
        for q, o in far:
            e_copy(c, q * 2 + core, me_i, o).wait_send()
            f_copy(c, q * 2 + core, o).wait_send()
            c_copy(c, q, o).wait_send()
        for q in range(n_q):
            b_copy(c, q).wait_send()
        z_copy(c).wait()
        return 0

    lax.fori_loop(0, n_ch, drain, 0)
    dpb_copy().wait_send()
    for q, o in far:
        dpc_copy(q, o).wait_send()
    for j in ep_peers:
        dpd_copy(j, me_j).wait_send()


def exchange(n_edp, n_ep, tokens, cotangent, gate_probs, expert_ids, w_gate, w_up, w_down):
    tok, width = tokens.shape
    hid = w_gate.shape[1]
    half = n_ep * CAP
    n_q = n_edp // 2
    n_far = max(n_q - 1, 1)
    n_ch = width // WIDE
    two = order_matrix(n_ep, 2)
    one = order_matrix(n_ep, 1)
    orders = [jnp.asarray(m, BF16) for m in (two, two.T, one, one.T)]
    vmem = pl.BlockSpec(memory_space=pltpu.VMEM)
    hbm = pl.BlockSpec(memory_space=pl.ANY)
    dma = pltpu.SemaphoreType.DMA
    rows = n_edp * 2 * half
    left = jax.ShapeDtypeStruct((hid, rows), BF16)
    return pl.pallas_call(
        functools.partial(main_kernel, n_edp, n_ep),
        out_shape=(
            jax.ShapeDtypeStruct((n_edp, 2 * half, width), BF16),
            left,
            left,
            left,
            jax.ShapeDtypeStruct((half, width), BF16),
            jax.ShapeDtypeStruct((half, tok), BF16),
            jax.ShapeDtypeStruct((gate_probs.shape[1], tok), BF16),
        ),
        in_specs=[hbm] * 2 + [vmem] * 2 + [hbm] * 3 + [vmem] * 4,
        out_specs=(hbm,) + (vmem,) * 6,
        scratch_shapes=[
            pltpu.VMEM((n_ch, tok, WIDE), BF16),
            pltpu.VMEM((n_ch, tok, WIDE), BF16),
            pltpu.VMEM((n_ch, 3 * hid, WIDE), BF16),
            pltpu.VMEM((n_ch, n_ep, SUB * 2 * CAP, LANES), BF16),
            pltpu.VMEM((n_ch, n_ep, SUB * 2 * CAP, LANES), BF16),
            pltpu.VMEM((n_ch, n_edp, 2 * half, WIDE), BF16),
            pltpu.VMEM((3 * hid, rows), F32),
            pltpu.VMEM((n_ch, n_edp, half, WIDE), BF16),
            pltpu.VMEM((n_ch, n_q, half, WIDE), BF16),
            pltpu.VMEM((n_ch, n_far, half, WIDE), BF16),
            pltpu.VMEM((n_ch, n_far, half, WIDE), BF16),
            pltpu.VMEM((n_ch, half, WIDE), F32),
            pltpu.VMEM((n_ch, n_ep, SUB * CAP, LANES), BF16),
            pltpu.VMEM((n_ch, n_ep, SUB * CAP, LANES), BF16),
            pltpu.VMEM((1, rows), F32),
            pltpu.VMEM((1, rows), F32),
            pltpu.VMEM((1, rows), F32),
            pltpu.VMEM((n_far, 1, rows), F32),
            pltpu.VMEM((1, rows), F32),
            pltpu.VMEM((n_ep, 1, rows), F32),
            dma((n_ch, 2)),
            dma((n_ch, 3)),
            dma((n_ch,)),
            dma((n_ch,)),
            dma((n_ch, n_ep)),
            dma((n_ch, n_ep)),
            dma((n_ch, n_q)),
            dma((n_ch, n_q)),
            dma((n_ch, n_q)),
            dma((n_ch, n_q)),
            dma((n_ch, n_q)),
            dma((n_ch, n_q)),
            dma((n_ch, n_far)),
            dma((n_ch, n_far)),
            dma((n_ch, n_ep)),
            dma((n_ch, n_ep)),
            dma((2,)),
            dma((n_far,)),
            dma((n_far,)),
            dma((n_ep,)),
            dma((n_ep,)),
        ],
        compiler_params=pltpu.CompilerParams(
            collective_id=0, has_side_effects=True, vmem_limit_bytes=60 * 2**20
        ),
    )(tokens, cotangent, gate_probs.T, expert_ids.T, w_gate, w_up, w_down, *orders)


def per_device(tokens, cotangent, gate_probs, expert_ids, w_gate, w_up, w_down):
    n_edp = lax.axis_size("edp")
    n_ep = lax.axis_size("ep")
    z, gate_left, up_left, down_left, back, live, gate_grad = exchange(
        n_edp, n_ep, tokens, cotangent, gate_probs, expert_ids, w_gate, w_up, w_down
    )
    rows = z.reshape(-1, z.shape[-1])
    weight_grads = [
        jnp.dot(left, rows, preferred_element_type=F32).astype(BF16)[None]
        for left in (gate_left, up_left, down_left)
    ]
    token_grad = lax.dot_general(live, back, TN, preferred_element_type=F32).astype(BF16)
    return (token_grad, gate_grad.T, *weight_grads)


def solution(mesh):
    rows = P(("edp", "ep"), None)
    weights = P("ep", "edp", None)
    return jax.shard_map(
        per_device,
        mesh=mesh,
        in_specs=(rows, rows, rows, rows, weights, weights, weights),
        out_specs=(rows, rows, weights, weights, weights),
        check_vma=False,
    )
```

```python
import functools

import jax
import jax.numpy as jnp
import numpy as np
from jax import lax
from jax.experimental import pallas as pl
from jax.experimental.pallas import tpu as pltpu
from jax.sharding import PartitionSpec as P

CAP = 3
LEAD = 3
NEAR = LEAD + 2
LAST = NEAR + 1
SUB = 8
LANES = 128
WIDE = SUB * LANES
MESH = pl.DeviceIdType.MESH
F32 = jnp.float32
BF16 = jnp.bfloat16
NT = (((1,), (1,)), ((), ()))
TN = (((0,), (0,)), ((), ()))


def order_matrix(n_ep, per):
    unit = CAP * per
    rows = n_ep * SUB * unit
    out = np.zeros((rows, rows), np.float32)
    for e in range(n_ep):
        for k in range(SUB):
            for kind in range(per):
                for s in range(CAP):
                    out[
                        (e * SUB + k) * unit + kind * CAP + s,
                        ((k * per + kind) * n_ep + e) * CAP + s,
                    ] = 1.0
    return out


def routes(ids, probs, columns):
    tok = ids.shape[1]
    row = lax.broadcasted_iota(jnp.int32, (columns, tok), 0)
    expert = row // CAP
    slot = row - expert * CAP
    match = jnp.zeros((columns, tok), F32)
    weight = jnp.zeros((columns, tok), F32)
    for r in range(ids.shape[0]):
        here = ids[r : r + 1] == expert
        match = jnp.where(here, 1.0, match)
        weight = jnp.where(here, probs[r : r + 1], weight)
    first = lax.broadcasted_iota(jnp.int32, (tok, tok), 0)
    second = lax.broadcasted_iota(jnp.int32, (tok, tok), 1)
    earlier = jnp.where(first < second, 1.0, 0.0).astype(BF16)
    before = jnp.dot(match.astype(BF16), earlier, preferred_element_type=F32)
    live = jnp.where(before == slot.astype(F32), match, 0.0)
    return live, live * weight


def main_kernel(
    n_edp, n_ep,
    tok_ref, cot_ref, probs_ref, ids_ref, wg_ref, wu_ref, wd_ref, ord2_ref, ord2t_ref, ord1_ref, ord1t_ref,
    z_out, gate_out, up_out, down_out, back_out, live_out, gg_out,
    tok, cot, w, send_a, recv_a, z, acc, send_b, recv_b, send_c, recv_c, own, send_d, recv_d,
    dp, dp_b, dp_s, dp_c, dp_d, dp_r,
    t_sem, w_sem, z_sem, loc_sem, a_ss, a_rs, e_ss, e_rs, f_ss, f_rs, b_ss, b_rs, c_ss, c_rs, d_ss, d_rs,
    pb_s, pc_ss, pc_rs, pd_ss, pd_rs,
):
    n_ch = z.shape[0]
    hid = wg_ref.shape[1]
    half = n_ep * CAP
    n_q = n_edp // 2
    me_i = lax.axis_index("edp")
    me_j = lax.axis_index("ep")
    q_me = me_i // 2
    core = me_i - q_me * 2
    mate = q_me * 2 + 1 - core

    def w_copy(c, part):
        src = (wg_ref, wu_ref, wd_ref)[part]
        return pltpu.make_async_copy(
            src.at[0, :, pl.ds(pl.multiple_of(c * WIDE, WIDE), WIDE)],
            w.at[c, pl.ds(part * hid, hid), :],
            w_sem.at[c, part],
        )

    def t_copy(c, part):
        src, dst = ((tok_ref, tok), (cot_ref, cot))[part]
        return pltpu.make_async_copy(
            src.at[:, pl.ds(pl.multiple_of(c * WIDE, WIDE), WIDE)], dst.at[c], t_sem.at[c, part]
        )

    for c in range(n_ch):
        t_copy(c, 0).start()
        t_copy(c, 1).start()

    barrier = pltpu.get_barrier_semaphore()
    ep_peers = [lax.rem(me_j + o, n_ep) for o in range(1, n_ep)]
    far = [(lax.rem(q_me + o, n_q), o) for o in range(1, n_q)]
    for j in ep_peers:
        pl.semaphore_signal(barrier, inc=1, device_id=(me_i, j), device_id_type=MESH)
    for q, _ in far:
        pl.semaphore_signal(barrier, inc=1, device_id=(q * 2 + core, me_j), device_id_type=MESH)
    pl.semaphore_signal(barrier, inc=1, device_id=(mate, me_j), device_id_type=MESH)

    live, scaled = routes(ids_ref[...], probs_ref[...].astype(F32), half)
    live_out[...] = live.astype(BF16)
    live_t = live.astype(BF16)
    scaled_t = scaled.astype(BF16)
    prob = jnp.sum(scaled, axis=1, keepdims=True)

    pl.semaphore_wait(barrier, n_ep - 1 + n_q - 1 + 1)

    def remote(src, dst, ss, rs, i, j):
        return pltpu.make_async_remote_copy(
            src_ref=src, dst_ref=dst, send_sem=ss, recv_sem=rs, device_id=(i, j), device_id_type=MESH
        )

    def a_copy(c, j, slot):
        return remote(send_a.at[c, j], recv_a.at[c, slot], a_ss.at[c, j], a_rs.at[c, slot], me_i, j)

    def a_own(c):
        return pltpu.make_async_copy(send_a.at[c, me_j], recv_a.at[c, me_j], loc_sem.at[c])

    def pack(c):
        t_copy(c, 0).wait()
        t_copy(c, 1).wait()
        x = jnp.dot(live_t, tok[c], preferred_element_type=F32)
        y = jnp.dot(scaled_t, cot[c], preferred_element_type=F32)
        parts = []
        for k in range(SUB):
            lanes = slice(k * LANES, (k + 1) * LANES)
            parts += [x[:, lanes], y[:, lanes]]
        mixed = jnp.concatenate(parts, axis=0).astype(BF16)
        packed = jnp.dot(ord2_ref[...], mixed, preferred_element_type=F32)
        send_a[c] = packed.astype(BF16).reshape(send_a.shape[1:])
        for j in ep_peers:
            a_copy(c, j, me_j).start()
        a_own(c).start()
        for part in range(3):
            w_copy(c, part).start()


    def e_copy(c, i, slot, o):
        return remote(z.at[c, me_i], z.at[c, slot], e_ss.at[c, o], e_rs.at[c, o], i, me_j)

    def f_copy(c, slot, o):
        return remote(z.at[c, slot], z.at[c, slot], f_ss.at[c, o], f_rs.at[c, o], mate, me_j)

    def gather(t, _):
        @pl.when(t < n_ch)
        def _():
            pack(t)

        @pl.when((t >= LEAD) & (t < n_ch + LEAD))
        def _():
            c = t - LEAD
            for j in ep_peers:
                a_copy(c, j, j).wait_recv()
            a_own(c).wait()
            mixed = recv_a[c].reshape(ord2_ref.shape[0], LANES)
            rows = jnp.dot(ord2t_ref[...], mixed, preferred_element_type=F32)
            wide = jnp.concatenate(
                [rows[k * 2 * half : (k + 1) * 2 * half] for k in range(SUB)], axis=1
            )
            z[c, me_i] = wide.astype(BF16)
            for q, o in far:
                e_copy(c, q * 2 + core, me_i, o).start()
            e_copy(c, mate, me_i, 0).start()

        @pl.when((t >= NEAR) & (t < n_ch + NEAR))
        def _():
            c = t - NEAR
            for _, o in far:
                from_q = lax.rem(q_me - o + n_q, n_q)
                e_copy(c, from_q * 2 + core, from_q * 2 + core, o).wait_recv()
                f_copy(c, from_q * 2 + core, o).start()

        @pl.when(t >= LAST)
        def _():
            c = t - LAST
            e_copy(c, mate, mate, 0).wait_recv()
            for _, o in far:
                from_q = lax.rem(q_me - o + n_q, n_q)
                f_copy(c, from_q * 2 + 1 - core, o).wait_recv()
            for part in range(3):
                w_copy(c, part).wait()
            rows = z[c].reshape(n_edp * 2 * half, WIDE)
            part = lax.dot_general(w[c], rows, NT, preferred_element_type=F32)

            @pl.when(c == 0)
            def _():
                acc[...] = part

            @pl.when(c > 0)
            def _():
                acc[...] += part

        return 0

    lax.fori_loop(0, n_ch + LAST, gather, 0)

    def z_copy(c):
        return pltpu.make_async_copy(
            z.at[c], z_out.at[:, :, pl.ds(pl.multiple_of(c * WIDE, WIDE), WIDE)], z_sem.at[c]
        )

    def z_start(c, _):
        z_copy(c).start()
        return 0

    lax.fori_loop(0, n_ch, z_start, 0)

    n_rows = n_edp * 2 * half
    a = acc[:hid]
    u = acc[hid : 2 * hid]
    g = pltpu.roll(acc[2 * hid :], n_rows - half, 1)
    lane = lax.broadcasted_iota(jnp.int32, (hid, n_rows), 1)
    is_x = lax.rem(lane // half, 2) == 0
    s = jax.nn.sigmoid(a)
    h = a * s * u
    d_a = jnp.where(is_x, g * u * s * (1.0 + a * (1.0 - s)), 0.0)
    d_u = jnp.where(is_x, g * a * s, 0.0)
    acc[:hid] = d_a
    acc[hid : 2 * hid] = d_u
    acc[2 * hid :] = jnp.where(is_x, h, 0.0)
    dp[...] = jnp.sum(jnp.where(is_x, h * g, 0.0), axis=0, keepdims=True)
    turned = acc[: 2 * hid].T
    both = jnp.concatenate(
        [turned[i * 2 * half : (i * 2 + 1) * half] for i in range(n_edp)], axis=0
    ).astype(BF16)

    def b_copy(c, q):
        return remote(
            send_b.at[c, q * 2 + 1 - core], recv_b.at[c, q], b_ss.at[c, q], b_rs.at[c, q], mate, me_j
        )

    def dpb_copy():
        return remote(dp, dp_b, pb_s.at[0], pb_s.at[1], mate, me_j)

    def c_copy(c, q, o):
        return remote(
            send_c.at[c, o - 1], recv_c.at[c, o - 1], c_ss.at[c, o - 1], c_rs.at[c, o - 1], q * 2 + core, me_j
        )

    def dpc_copy(q, o):
        return remote(dp_s, dp_c.at[o - 1], pc_ss.at[o - 1], pc_rs.at[o - 1], q * 2 + core, me_j)

    def d_copy(c, j, slot):
        return remote(send_d.at[c, j], recv_d.at[c, slot], d_ss.at[c, j], d_rs.at[c, slot], me_i, j)

    def dpd_copy(j, slot):
        return remote(dp_d, dp_r.at[slot], pd_ss.at[j], pd_rs.at[slot], me_i, j)

    dpb_copy().start()

    def give_back(t, _):
        @pl.when(t < n_ch)
        def _():
            c = t
            part = jnp.dot(both, w[c, : 2 * hid, :], preferred_element_type=F32)
            for i in range(n_edp):
                send_b[c, i] = part[i * half : (i + 1) * half].astype(BF16)
            for q in range(n_q):
                b_copy(c, q).start()

        @pl.when((t >= 2) & (t < n_ch + 2))
        def _():
            c = t - 2
            for q in range(n_q):
                b_copy(c, q).wait_recv()
            for q, o in far:
                total = send_b[c, q * 2 + core].astype(F32) + recv_b[c, q].astype(F32)
                send_c[c, o - 1] = total.astype(BF16)
                c_copy(c, q, o).start()
            own[c] = send_b[c, me_i].astype(F32) + recv_b[c, q_me].astype(F32)

            @pl.when(c == 0)
            def _():
                dpb_copy().wait_recv()
                dp_s[...] = dp[...] + dp_b[...]
                for q, o in far:
                    dpc_copy(q, o).start()

        @pl.when(t >= 4)
        def _():
            c = t - 4
            total = own[c]
            for q, o in far:
                c_copy(c, q, o).wait_recv()
                total = total + recv_c[c, o - 1].astype(F32)
            mixed = jnp.concatenate(
                [total[:, k * LANES : (k + 1) * LANES] for k in range(SUB)], axis=0
            ).astype(BF16)
            packed = jnp.dot(ord1_ref[...], mixed, preferred_element_type=F32)
            send_d[c] = packed.astype(BF16).reshape(send_d.shape[1:])
            for j in ep_peers:
                d_copy(c, j, me_j).start()
            recv_d[c, me_j] = send_d[c, me_j]

            @pl.when(c == 0)
            def _():
                whole_dp = dp_s[...]
                for q, o in far:
                    dpc_copy(q, o).wait_recv()
                    whole_dp = whole_dp + dp_c[o - 1]
                dp_d[...] = whole_dp
                dp_r[me_j] = whole_dp
                for j in ep_peers:
                    dpd_copy(j, me_j).start()

        return 0

    lax.fori_loop(0, n_ch + 4, give_back, 0)

    spin = pltpu.roll(acc[2 * hid :], half, 1)
    gate_out[...] = acc[:hid].astype(BF16)
    up_out[...] = acc[hid : 2 * hid].astype(BF16)
    down_out[...] = spin.astype(BF16)

    def finish(c, _):
        for j in ep_peers:
            d_copy(c, j, j).wait_recv()
        mixed = recv_d[c].reshape(ord1_ref.shape[0], LANES)
        rows = jnp.dot(ord1t_ref[...], mixed, preferred_element_type=F32)
        wide = jnp.concatenate([rows[k * half : (k + 1) * half] for k in range(SUB)], axis=1)
        back_out[:, pl.ds(pl.multiple_of(c * WIDE, WIDE), WIDE)] = wide.astype(BF16)
        return 0

    lax.fori_loop(0, n_ch, finish, 0)

    for j in ep_peers:
        dpd_copy(j, j).wait_recv()
    at = lax.broadcasted_iota(jnp.int32, (1, n_rows), 1) - (me_i * 2 * half + me_j * CAP)
    row = lax.broadcasted_iota(jnp.int32, (half, 1), 0)
    got = jnp.zeros((half, 1), F32)
    for e in range(n_ep):
        for slot in range(CAP):
            value = jnp.sum(jnp.where(at == slot, dp_r[e], 0.0), axis=1, keepdims=True)
            got = jnp.where(row == e * CAP + slot, value, got)
    got = jnp.where(prob > 0.0, got / jnp.where(prob > 0.0, prob, 1.0), 0.0)
    got = got.astype(BF16).astype(F32)
    value = live * got
    owner = lax.broadcasted_iota(jnp.int32, live.shape, 0) // CAP
    grads = []
    for r in range(ids_ref.shape[0]):
        mine = jnp.where(ids_ref[r : r + 1] == owner, value, 0.0)
        grads.append(jnp.sum(mine, axis=0, keepdims=True))
    gg_out[...] = jnp.concatenate(grads, axis=0).astype(BF16)

    def drain(c, _):
        for j in ep_peers:
            a_copy(c, j, me_j).wait_send()
            d_copy(c, j, me_j).wait_send()
        e_copy(c, mate, me_i, 0).wait_send()
        for q, o in far:
            e_copy(c, q * 2 + core, me_i, o).wait_send()
            f_copy(c, q * 2 + core, o).wait_send()
            c_copy(c, q, o).wait_send()
        for q in range(n_q):
            b_copy(c, q).wait_send()
        z_copy(c).wait()
        return 0

    lax.fori_loop(0, n_ch, drain, 0)
    dpb_copy().wait_send()
    for q, o in far:
        dpc_copy(q, o).wait_send()
    for j in ep_peers:
        dpd_copy(j, me_j).wait_send()


def exchange(n_edp, n_ep, tokens, cotangent, gate_probs, expert_ids, w_gate, w_up, w_down):
    tok, width = tokens.shape
    hid = w_gate.shape[1]
    half = n_ep * CAP
    n_q = n_edp // 2
    n_far = max(n_q - 1, 1)
    n_ch = width // WIDE
    two = order_matrix(n_ep, 2)
    one = order_matrix(n_ep, 1)
    orders = [jnp.asarray(m, BF16) for m in (two, two.T, one, one.T)]
    vmem = pl.BlockSpec(memory_space=pltpu.VMEM)
    hbm = pl.BlockSpec(memory_space=pl.ANY)
    dma = pltpu.SemaphoreType.DMA
    rows = n_edp * 2 * half
    left = jax.ShapeDtypeStruct((hid, rows), BF16)
    return pl.pallas_call(
        functools.partial(main_kernel, n_edp, n_ep),
        out_shape=(
            jax.ShapeDtypeStruct((n_edp, 2 * half, width), BF16),
            left,
            left,
            left,
            jax.ShapeDtypeStruct((half, width), BF16),
            jax.ShapeDtypeStruct((half, tok), BF16),
            jax.ShapeDtypeStruct((gate_probs.shape[1], tok), BF16),
        ),
        in_specs=[hbm] * 2 + [vmem] * 2 + [hbm] * 3 + [vmem] * 4,
        out_specs=(hbm,) + (vmem,) * 6,
        scratch_shapes=[
            pltpu.VMEM((n_ch, tok, WIDE), BF16),
            pltpu.VMEM((n_ch, tok, WIDE), BF16),
            pltpu.VMEM((n_ch, 3 * hid, WIDE), BF16),
            pltpu.VMEM((n_ch, n_ep, SUB * 2 * CAP, LANES), BF16),
            pltpu.VMEM((n_ch, n_ep, SUB * 2 * CAP, LANES), BF16),
            pltpu.VMEM((n_ch, n_edp, 2 * half, WIDE), BF16),
            pltpu.VMEM((3 * hid, rows), F32),
            pltpu.VMEM((n_ch, n_edp, half, WIDE), BF16),
            pltpu.VMEM((n_ch, n_q, half, WIDE), BF16),
            pltpu.VMEM((n_ch, n_far, half, WIDE), BF16),
            pltpu.VMEM((n_ch, n_far, half, WIDE), BF16),
            pltpu.VMEM((n_ch, half, WIDE), F32),
            pltpu.VMEM((n_ch, n_ep, SUB * CAP, LANES), BF16),
            pltpu.VMEM((n_ch, n_ep, SUB * CAP, LANES), BF16),
            pltpu.VMEM((1, rows), F32),
            pltpu.VMEM((1, rows), F32),
            pltpu.VMEM((1, rows), F32),
            pltpu.VMEM((n_far, 1, rows), F32),
            pltpu.VMEM((1, rows), F32),
            pltpu.VMEM((n_ep, 1, rows), F32),
            dma((n_ch, 2)),
            dma((n_ch, 3)),
            dma((n_ch,)),
            dma((n_ch,)),
            dma((n_ch, n_ep)),
            dma((n_ch, n_ep)),
            dma((n_ch, n_q)),
            dma((n_ch, n_q)),
            dma((n_ch, n_q)),
            dma((n_ch, n_q)),
            dma((n_ch, n_q)),
            dma((n_ch, n_q)),
            dma((n_ch, n_far)),
            dma((n_ch, n_far)),
            dma((n_ch, n_ep)),
            dma((n_ch, n_ep)),
            dma((2,)),
            dma((n_far,)),
            dma((n_far,)),
            dma((n_ep,)),
            dma((n_ep,)),
        ],
        compiler_params=pltpu.CompilerParams(
            collective_id=0, has_side_effects=True, vmem_limit_bytes=60 * 2**20
        ),
    )(tokens, cotangent, gate_probs.T, expert_ids.T, w_gate, w_up, w_down, *orders)


def grads_kernel(z_ref, gl_ref, ul_ref, dl_ref, back_ref, live_ref, gg_ref, tg_out, gg_out, wg_out, wu_out, wd_out):
    rows = z_ref[...].reshape(gl_ref.shape[1], z_ref.shape[2])
    for left, out in ((gl_ref, wg_out), (ul_ref, wu_out), (dl_ref, wd_out)):
        out[0] = jnp.dot(left[...], rows, preferred_element_type=F32).astype(BF16)
    tg_out[...] = lax.dot_general(
        live_ref[...], back_ref[...], TN, preferred_element_type=F32
    ).astype(BF16)
    gg_out[...] = gg_ref[...]


def per_device(tokens, cotangent, gate_probs, expert_ids, w_gate, w_up, w_down):
    n_edp = lax.axis_size("edp")
    n_ep = lax.axis_size("ep")
    half = n_ep * CAP
    results = exchange(
        n_edp, n_ep, tokens, cotangent, gate_probs, expert_ids, w_gate, w_up, w_down
    )
    tok, width = tokens.shape
    hid = w_gate.shape[1]
    rows = n_edp * 2 * half
    step = WIDE // 2
    top = gate_probs.shape[1]

    def whole(*shape):
        return pl.BlockSpec(shape, lambda c: (0,) * len(shape))

    w_spec = pl.BlockSpec((1, hid, step), lambda c: (0, 0, c))
    w_shape = jax.ShapeDtypeStruct(w_gate.shape, BF16)
    token_grad, gate_grad, *weight_grads = pl.pallas_call(
        grads_kernel,
        grid=(width // step,),
        out_shape=(
            jax.ShapeDtypeStruct((tok, width), BF16),
            jax.ShapeDtypeStruct((top, tok), BF16),
            w_shape,
            w_shape,
            w_shape,
        ),
        in_specs=[
            pl.BlockSpec((n_edp, 2 * half, step), lambda c: (0, 0, c)),
            whole(hid, rows),
            whole(hid, rows),
            whole(hid, rows),
            pl.BlockSpec((half, step), lambda c: (0, c)),
            whole(half, tok),
            whole(top, tok),
        ],
        out_specs=(
            pl.BlockSpec((tok, step), lambda c: (0, c)),
            whole(top, tok),
            w_spec,
            w_spec,
            w_spec,
        ),
        compiler_params=pltpu.CompilerParams(vmem_limit_bytes=63 * 2**20),
    )(*results)
    return (token_grad, gate_grad.T, *weight_grads)


def solution(mesh):
    rows = P(("edp", "ep"), None)
    weights = P("ep", "edp", None)
    return jax.shard_map(
        per_device,
        mesh=mesh,
        in_specs=(rows, rows, rows, rows, weights, weights, weights),
        out_specs=(rows, rows, weights, weights, weights),
        check_vma=False,
    )
```

```python
import functools

import jax
import jax.numpy as jnp
import numpy as np
from jax import lax
from jax.experimental import pallas as pl
from jax.experimental.pallas import tpu as pltpu
from jax.sharding import PartitionSpec as P

CAP = 3
LEAD = 3
NEAR = LEAD + 2
LAST = NEAR + 1
SUB = 8
LANES = 128
WIDE = SUB * LANES
MESH = pl.DeviceIdType.MESH
F32 = jnp.float32
BF16 = jnp.bfloat16
NT = (((1,), (1,)), ((), ()))
TN = (((0,), (0,)), ((), ()))


def order_matrix(n_ep, per):
    unit = CAP * per
    rows = n_ep * SUB * unit
    out = np.zeros((rows, rows), np.float32)
    for e in range(n_ep):
        for k in range(SUB):
            for kind in range(per):
                for s in range(CAP):
                    out[
                        (e * SUB + k) * unit + kind * CAP + s,
                        ((k * per + kind) * n_ep + e) * CAP + s,
                    ] = 1.0
    return out


def routes(ids, probs, columns):
    tok = ids.shape[1]
    row = lax.broadcasted_iota(jnp.int32, (columns, tok), 0)
    expert = row // CAP
    slot = row - expert * CAP
    match = jnp.zeros((columns, tok), F32)
    weight = jnp.zeros((columns, tok), F32)
    for r in range(ids.shape[0]):
        here = ids[r : r + 1] == expert
        match = jnp.where(here, 1.0, match)
        weight = jnp.where(here, probs[r : r + 1], weight)
    first = lax.broadcasted_iota(jnp.int32, (tok, tok), 0)
    second = lax.broadcasted_iota(jnp.int32, (tok, tok), 1)
    earlier = jnp.where(first < second, 1.0, 0.0).astype(BF16)
    before = jnp.dot(match.astype(BF16), earlier, preferred_element_type=F32)
    live = jnp.where(before == slot.astype(F32), match, 0.0)
    return live, live * weight


def main_kernel(
    n_edp, n_ep,
    tok_ref, cot_ref, probs_ref, ids_ref, wg_ref, wu_ref, wd_ref, ord2_in, ord2t_in, ord1_in, ord1t_in,
    z_out, left_out, back_out, live_out, gg_out,
    ord2_ref, ord2t_ref, ord1_ref, ord1t_ref, left, tok, cot, w, send_a, recv_a, z, acc, send_b, recv_b, send_c, recv_c, own, send_d, recv_d,
    dp, dp_b, dp_s, dp_c, dp_d, dp_r,
    o_sem, l_sem, t_sem, w_sem, z_sem, loc_sem, a_ss, a_rs, e_ss, e_rs, f_ss, f_rs, b_ss, b_rs, c_ss, c_rs, d_ss, d_rs,
    pb_s, pc_ss, pc_rs, pd_ss, pd_rs,
):
    n_ch = z.shape[0]
    hid = wg_ref.shape[1]
    half = n_ep * CAP
    n_q = n_edp // 2
    me_i = lax.axis_index("edp")
    me_j = lax.axis_index("ep")
    q_me = me_i // 2
    core = me_i - q_me * 2
    mate = q_me * 2 + 1 - core

    def w_copy(c, part):
        src = (wg_ref, wu_ref, wd_ref)[part]
        return pltpu.make_async_copy(
            src.at[0, :, pl.ds(pl.multiple_of(c * WIDE, WIDE), WIDE)],
            w.at[c, pl.ds(part * hid, hid), :],
            w_sem.at[c, part],
        )

    def t_copy(c, part):
        src, dst = ((tok_ref, tok), (cot_ref, cot))[part]
        return pltpu.make_async_copy(
            src.at[:, pl.ds(pl.multiple_of(c * WIDE, WIDE), WIDE)], dst.at[c], t_sem.at[c, part]
        )

    o_copies = [
        pltpu.make_async_copy(src, dst, o_sem.at[k])
        for k, (src, dst) in enumerate(
            ((ord2_in, ord2_ref), (ord2t_in, ord2t_ref), (ord1_in, ord1_ref), (ord1t_in, ord1t_ref))
        )
    ]
    for c in range(n_ch):
        t_copy(c, 0).start()
        t_copy(c, 1).start()
        if c < len(o_copies):
            o_copies[c].start()

    barrier = pltpu.get_barrier_semaphore()
    ep_peers = [lax.rem(me_j + o, n_ep) for o in range(1, n_ep)]
    far = [(lax.rem(q_me + o, n_q), o) for o in range(1, n_q)]
    for j in ep_peers:
        pl.semaphore_signal(barrier, inc=1, device_id=(me_i, j), device_id_type=MESH)
    for q, _ in far:
        pl.semaphore_signal(barrier, inc=1, device_id=(q * 2 + core, me_j), device_id_type=MESH)
    pl.semaphore_signal(barrier, inc=1, device_id=(mate, me_j), device_id_type=MESH)

    live, scaled = routes(ids_ref[...], probs_ref[...].astype(F32), half)
    live_out[...] = live.astype(BF16)
    live_t = live.astype(BF16)
    scaled_t = scaled.astype(BF16)
    prob = jnp.sum(scaled, axis=1, keepdims=True)

    for copy in o_copies:
        copy.wait()
    pl.semaphore_wait(barrier, n_ep - 1 + n_q - 1 + 1)

    def remote(src, dst, ss, rs, i, j):
        return pltpu.make_async_remote_copy(
            src_ref=src, dst_ref=dst, send_sem=ss, recv_sem=rs, device_id=(i, j), device_id_type=MESH
        )

    def a_copy(c, j, slot):
        return remote(send_a.at[c, j], recv_a.at[c, slot], a_ss.at[c, j], a_rs.at[c, slot], me_i, j)

    def a_own(c):
        return pltpu.make_async_copy(send_a.at[c, me_j], recv_a.at[c, me_j], loc_sem.at[c])

    def pack(c):
        t_copy(c, 0).wait()
        t_copy(c, 1).wait()
        x = jnp.dot(live_t, tok[c], preferred_element_type=F32)
        y = jnp.dot(scaled_t, cot[c], preferred_element_type=F32)
        parts = []
        for k in range(SUB):
            lanes = slice(k * LANES, (k + 1) * LANES)
            parts += [x[:, lanes], y[:, lanes]]
        mixed = jnp.concatenate(parts, axis=0).astype(BF16)
        packed = jnp.dot(ord2_ref[...], mixed, preferred_element_type=F32)
        send_a[c] = packed.astype(BF16).reshape(send_a.shape[1:])
        for j in ep_peers:
            a_copy(c, j, me_j).start()
        a_own(c).start()
        for part in range(3):
            w_copy(c, part).start()


    def e_copy(c, i, slot, o):
        return remote(z.at[c, me_i], z.at[c, slot], e_ss.at[c, o], e_rs.at[c, o], i, me_j)

    def f_copy(c, slot, o):
        return remote(z.at[c, slot], z.at[c, slot], f_ss.at[c, o], f_rs.at[c, o], mate, me_j)

    def gather(t, _):
        @pl.when(t < n_ch)
        def _():
            pack(t)

        @pl.when((t >= LEAD) & (t < n_ch + LEAD))
        def _():
            c = t - LEAD
            for j in ep_peers:
                a_copy(c, j, j).wait_recv()
            a_own(c).wait()
            mixed = recv_a[c].reshape(ord2_ref.shape[0], LANES)
            rows = jnp.dot(ord2t_ref[...], mixed, preferred_element_type=F32)
            wide = jnp.concatenate(
                [rows[k * 2 * half : (k + 1) * 2 * half] for k in range(SUB)], axis=1
            )
            z[c, me_i] = wide.astype(BF16)
            for q, o in far:
                e_copy(c, q * 2 + core, me_i, o).start()
            e_copy(c, mate, me_i, 0).start()

        @pl.when((t >= NEAR) & (t < n_ch + NEAR))
        def _():
            c = t - NEAR
            for _, o in far:
                from_q = lax.rem(q_me - o + n_q, n_q)
                e_copy(c, from_q * 2 + core, from_q * 2 + core, o).wait_recv()
                f_copy(c, from_q * 2 + core, o).start()

        @pl.when(t >= LAST)
        def _():
            c = t - LAST
            e_copy(c, mate, mate, 0).wait_recv()
            for _, o in far:
                from_q = lax.rem(q_me - o + n_q, n_q)
                f_copy(c, from_q * 2 + 1 - core, o).wait_recv()
            for part in range(3):
                w_copy(c, part).wait()
            rows = z[c].reshape(n_edp * 2 * half, WIDE)
            part = lax.dot_general(w[c], rows, NT, preferred_element_type=F32)

            @pl.when(c == 0)
            def _():
                acc[...] = part

            @pl.when(c > 0)
            def _():
                acc[...] += part

        return 0

    lax.fori_loop(0, n_ch + LAST, gather, 0)

    def z_copy(c):
        return pltpu.make_async_copy(
            z.at[c], z_out.at[:, :, pl.ds(pl.multiple_of(c * WIDE, WIDE), WIDE)], z_sem.at[c]
        )

    def z_start(c, _):
        z_copy(c).start()
        return 0

    lax.fori_loop(0, n_ch, z_start, 0)

    n_rows = n_edp * 2 * half
    a = acc[:hid]
    u = acc[hid : 2 * hid]
    g = pltpu.roll(acc[2 * hid :], n_rows - half, 1)
    lane = lax.broadcasted_iota(jnp.int32, (hid, n_rows), 1)
    is_x = lax.rem(lane // half, 2) == 0
    s = jax.nn.sigmoid(a)
    h = a * s * u
    d_a = jnp.where(is_x, g * u * s * (1.0 + a * (1.0 - s)), 0.0)
    d_u = jnp.where(is_x, g * a * s, 0.0)
    acc[:hid] = d_a
    acc[hid : 2 * hid] = d_u
    acc[2 * hid :] = jnp.where(is_x, h, 0.0)
    dp[...] = jnp.sum(jnp.where(is_x, h * g, 0.0), axis=0, keepdims=True)
    turned = acc[: 2 * hid].T
    both = jnp.concatenate(
        [turned[i * 2 * half : (i * 2 + 1) * half] for i in range(n_edp)], axis=0
    ).astype(BF16)

    def b_copy(c, q):
        return remote(
            send_b.at[c, q * 2 + 1 - core], recv_b.at[c, q], b_ss.at[c, q], b_rs.at[c, q], mate, me_j
        )

    def dpb_copy():
        return remote(dp, dp_b, pb_s.at[0], pb_s.at[1], mate, me_j)

    def c_copy(c, q, o):
        return remote(
            send_c.at[c, o - 1], recv_c.at[c, o - 1], c_ss.at[c, o - 1], c_rs.at[c, o - 1], q * 2 + core, me_j
        )

    def dpc_copy(q, o):
        return remote(dp_s, dp_c.at[o - 1], pc_ss.at[o - 1], pc_rs.at[o - 1], q * 2 + core, me_j)

    def d_copy(c, j, slot):
        return remote(send_d.at[c, j], recv_d.at[c, slot], d_ss.at[c, j], d_rs.at[c, slot], me_i, j)

    def dpd_copy(j, slot):
        return remote(dp_d, dp_r.at[slot], pd_ss.at[j], pd_rs.at[slot], me_i, j)

    dpb_copy().start()

    def give_back(t, _):
        @pl.when(t < n_ch)
        def _():
            c = t
            part = jnp.dot(both, w[c, : 2 * hid, :], preferred_element_type=F32)
            for i in range(n_edp):
                send_b[c, i] = part[i * half : (i + 1) * half].astype(BF16)
            for q in range(n_q):
                b_copy(c, q).start()

        @pl.when((t >= 2) & (t < n_ch + 2))
        def _():
            c = t - 2
            for q in range(n_q):
                b_copy(c, q).wait_recv()
            for q, o in far:
                total = send_b[c, q * 2 + core].astype(F32) + recv_b[c, q].astype(F32)
                send_c[c, o - 1] = total.astype(BF16)
                c_copy(c, q, o).start()
            own[c] = send_b[c, me_i].astype(F32) + recv_b[c, q_me].astype(F32)

            @pl.when(c == 0)
            def _():
                dpb_copy().wait_recv()
                dp_s[...] = dp[...] + dp_b[...]
                for q, o in far:
                    dpc_copy(q, o).start()

        @pl.when(t >= 4)
        def _():
            c = t - 4
            total = own[c]
            for q, o in far:
                c_copy(c, q, o).wait_recv()
                total = total + recv_c[c, o - 1].astype(F32)
            mixed = jnp.concatenate(
                [total[:, k * LANES : (k + 1) * LANES] for k in range(SUB)], axis=0
            ).astype(BF16)
            packed = jnp.dot(ord1_ref[...], mixed, preferred_element_type=F32)
            send_d[c] = packed.astype(BF16).reshape(send_d.shape[1:])
            for j in ep_peers:
                d_copy(c, j, me_j).start()
            recv_d[c, me_j] = send_d[c, me_j]

            @pl.when(c == 0)
            def _():
                whole_dp = dp_s[...]
                for q, o in far:
                    dpc_copy(q, o).wait_recv()
                    whole_dp = whole_dp + dp_c[o - 1]
                dp_d[...] = whole_dp
                dp_r[me_j] = whole_dp
                for j in ep_peers:
                    dpd_copy(j, me_j).start()

        return 0

    lax.fori_loop(0, n_ch + 4, give_back, 0)

    spin = pltpu.roll(acc[2 * hid :], half, 1)
    left[: 2 * hid] = acc[: 2 * hid].astype(BF16)
    left[2 * hid :] = spin.astype(BF16)
    left_copy = pltpu.make_async_copy(left, left_out, l_sem)
    left_copy.start()

    def finish(c, _):
        for j in ep_peers:
            d_copy(c, j, j).wait_recv()
        mixed = recv_d[c].reshape(ord1_ref.shape[0], LANES)
        rows = jnp.dot(ord1t_ref[...], mixed, preferred_element_type=F32)
        wide = jnp.concatenate([rows[k * half : (k + 1) * half] for k in range(SUB)], axis=1)
        back_out[:, pl.ds(pl.multiple_of(c * WIDE, WIDE), WIDE)] = wide.astype(BF16)
        return 0

    lax.fori_loop(0, n_ch, finish, 0)

    for j in ep_peers:
        dpd_copy(j, j).wait_recv()
    at = lax.broadcasted_iota(jnp.int32, (1, n_rows), 1) - (me_i * 2 * half + me_j * CAP)
    row = lax.broadcasted_iota(jnp.int32, (half, 1), 0)
    got = jnp.zeros((half, 1), F32)
    for e in range(n_ep):
        for slot in range(CAP):
            value = jnp.sum(jnp.where(at == slot, dp_r[e], 0.0), axis=1, keepdims=True)
            got = jnp.where(row == e * CAP + slot, value, got)
    got = jnp.where(prob > 0.0, got / jnp.where(prob > 0.0, prob, 1.0), 0.0)
    got = got.astype(BF16).astype(F32)
    value = live * got
    owner = lax.broadcasted_iota(jnp.int32, live.shape, 0) // CAP
    grads = []
    for r in range(ids_ref.shape[0]):
        mine = jnp.where(ids_ref[r : r + 1] == owner, value, 0.0)
        grads.append(jnp.sum(mine, axis=0, keepdims=True))
    gg_out[...] = jnp.concatenate(grads, axis=0).astype(BF16)

    def drain(c, _):
        for j in ep_peers:
            a_copy(c, j, me_j).wait_send()
            d_copy(c, j, me_j).wait_send()
        e_copy(c, mate, me_i, 0).wait_send()
        for q, o in far:
            e_copy(c, q * 2 + core, me_i, o).wait_send()
            f_copy(c, q * 2 + core, o).wait_send()
            c_copy(c, q, o).wait_send()
        for q in range(n_q):
            b_copy(c, q).wait_send()
        z_copy(c).wait()
        return 0

    lax.fori_loop(0, n_ch, drain, 0)
    left_copy.wait()
    dpb_copy().wait_send()
    for q, o in far:
        dpc_copy(q, o).wait_send()
    for j in ep_peers:
        dpd_copy(j, me_j).wait_send()


def exchange(n_edp, n_ep, tokens, cotangent, gate_probs, expert_ids, w_gate, w_up, w_down):
    tok, width = tokens.shape
    hid = w_gate.shape[1]
    half = n_ep * CAP
    n_q = n_edp // 2
    n_far = max(n_q - 1, 1)
    n_ch = width // WIDE
    two = order_matrix(n_ep, 2)
    one = order_matrix(n_ep, 1)
    orders = [jnp.asarray(m, BF16) for m in (two, two.T, one, one.T)]
    vmem = pl.BlockSpec(memory_space=pltpu.VMEM)
    hbm = pl.BlockSpec(memory_space=pl.ANY)
    dma = pltpu.SemaphoreType.DMA
    rows = n_edp * 2 * half
    left = jax.ShapeDtypeStruct((3 * hid, rows), BF16)
    return pl.pallas_call(
        functools.partial(main_kernel, n_edp, n_ep),
        out_shape=(
            jax.ShapeDtypeStruct((n_edp, 2 * half, width), BF16),
            left,
            jax.ShapeDtypeStruct((half, width), BF16),
            jax.ShapeDtypeStruct((half, tok), BF16),
            jax.ShapeDtypeStruct((gate_probs.shape[1], tok), BF16),
        ),
        in_specs=[hbm] * 2 + [vmem] * 2 + [hbm] * 7,
        out_specs=(hbm,) * 2 + (vmem,) * 3,
        scratch_shapes=[
            *[pltpu.VMEM(m.shape, BF16) for m in orders],
            pltpu.VMEM((3 * hid, rows), BF16),
            pltpu.VMEM((n_ch, tok, WIDE), BF16),
            pltpu.VMEM((n_ch, tok, WIDE), BF16),
            pltpu.VMEM((n_ch, 3 * hid, WIDE), BF16),
            pltpu.VMEM((n_ch, n_ep, SUB * 2 * CAP, LANES), BF16),
            pltpu.VMEM((n_ch, n_ep, SUB * 2 * CAP, LANES), BF16),
            pltpu.VMEM((n_ch, n_edp, 2 * half, WIDE), BF16),
            pltpu.VMEM((3 * hid, rows), F32),
            pltpu.VMEM((n_ch, n_edp, half, WIDE), BF16),
            pltpu.VMEM((n_ch, n_q, half, WIDE), BF16),
            pltpu.VMEM((n_ch, n_far, half, WIDE), BF16),
            pltpu.VMEM((n_ch, n_far, half, WIDE), BF16),
            pltpu.VMEM((n_ch, half, WIDE), F32),
            pltpu.VMEM((n_ch, n_ep, SUB * CAP, LANES), BF16),
            pltpu.VMEM((n_ch, n_ep, SUB * CAP, LANES), BF16),
            pltpu.VMEM((1, rows), F32),
            pltpu.VMEM((1, rows), F32),
            pltpu.VMEM((1, rows), F32),
            pltpu.VMEM((n_far, 1, rows), F32),
            pltpu.VMEM((1, rows), F32),
            pltpu.VMEM((n_ep, 1, rows), F32),
            dma((len(orders),)),
            dma,
            dma((n_ch, 2)),
            dma((n_ch, 3)),
            dma((n_ch,)),
            dma((n_ch,)),
            dma((n_ch, n_ep)),
            dma((n_ch, n_ep)),
            dma((n_ch, n_q)),
            dma((n_ch, n_q)),
            dma((n_ch, n_q)),
            dma((n_ch, n_q)),
            dma((n_ch, n_q)),
            dma((n_ch, n_q)),
            dma((n_ch, n_far)),
            dma((n_ch, n_far)),
            dma((n_ch, n_ep)),
            dma((n_ch, n_ep)),
            dma((2,)),
            dma((n_far,)),
            dma((n_far,)),
            dma((n_ep,)),
            dma((n_ep,)),
        ],
        compiler_params=pltpu.CompilerParams(
            collective_id=0, has_side_effects=True, vmem_limit_bytes=60 * 2**20
        ),
    )(tokens, cotangent, gate_probs.T, expert_ids.T, w_gate, w_up, w_down, *orders)


def grads_kernel(
    z_in, left_in, back_in, live_ref, gg_ref,
    tg_out, gg_out, wg_out, wu_out, wd_out,
    z, left, back, grads, token, in_sem, left_sem, out_sem,
):
    n_ch = z.shape[0]
    hid = wg_out.shape[1]

    def columns(c):
        return pl.ds(c * WIDE, WIDE)

    def loads(c):
        return (
            pltpu.make_async_copy(z_in.at[:, :, columns(c)], z.at[c], in_sem.at[c, 0]),
            pltpu.make_async_copy(back_in.at[:, columns(c)], back.at[c], in_sem.at[c, 1]),
        )

    def stores(c):
        outs = [
            pltpu.make_async_copy(
                grads.at[c, pl.ds(part * hid, hid)], out.at[0, :, columns(c)], out_sem.at[c, part]
            )
            for part, out in enumerate((wg_out, wu_out, wd_out))
        ]
        outs.append(pltpu.make_async_copy(token.at[c], tg_out.at[:, columns(c)], out_sem.at[c, 3]))
        return outs

    left_copy = pltpu.make_async_copy(left_in, left, left_sem)
    left_copy.start()
    for c in range(n_ch):
        for copy in loads(c):
            copy.start()
    gg_out[...] = gg_ref[...]
    left_copy.wait()
    for c in range(n_ch):
        for copy in loads(c):
            copy.wait()
        rows = z[c].reshape(left.shape[1], WIDE)
        grads[c] = jnp.dot(left[...], rows, preferred_element_type=F32).astype(BF16)
        token[c] = lax.dot_general(
            live_ref[...], back[c], TN, preferred_element_type=F32
        ).astype(BF16)
        for copy in stores(c):
            copy.start()
    for c in range(n_ch):
        for copy in stores(c):
            copy.wait()


def per_device(tokens, cotangent, gate_probs, expert_ids, w_gate, w_up, w_down):
    n_edp = lax.axis_size("edp")
    n_ep = lax.axis_size("ep")
    half = n_ep * CAP
    results = exchange(
        n_edp, n_ep, tokens, cotangent, gate_probs, expert_ids, w_gate, w_up, w_down
    )
    tok, width = tokens.shape
    hid = w_gate.shape[1]
    rows = n_edp * 2 * half
    n_ch = width // WIDE
    vmem = pl.BlockSpec(memory_space=pltpu.VMEM)
    hbm = pl.BlockSpec(memory_space=pl.ANY)
    dma = pltpu.SemaphoreType.DMA
    w_shape = jax.ShapeDtypeStruct(w_gate.shape, BF16)
    token_grad, gate_grad, *weight_grads = pl.pallas_call(
        grads_kernel,
        out_shape=(
            jax.ShapeDtypeStruct((tok, width), BF16),
            jax.ShapeDtypeStruct((gate_probs.shape[1], tok), BF16),
            w_shape,
            w_shape,
            w_shape,
        ),
        in_specs=[hbm, hbm, hbm, vmem, vmem],
        out_specs=(hbm, vmem, hbm, hbm, hbm),
        scratch_shapes=[
            pltpu.VMEM((n_ch, n_edp, 2 * half, WIDE), BF16),
            pltpu.VMEM((3 * hid, rows), BF16),
            pltpu.VMEM((n_ch, half, WIDE), BF16),
            pltpu.VMEM((n_ch, 3 * hid, WIDE), BF16),
            pltpu.VMEM((n_ch, tok, WIDE), BF16),
            dma((n_ch, 2)),
            dma,
            dma((n_ch, 4)),
        ],
        compiler_params=pltpu.CompilerParams(vmem_limit_bytes=62 * 2**20),
    )(*results)
    return (token_grad, gate_grad.T, *weight_grads)


def solution(mesh):
    rows = P(("edp", "ep"), None)
    weights = P("ep", "edp", None)
    return jax.shard_map(
        per_device,
        mesh=mesh,
        in_specs=(rows, rows, rows, rows, weights, weights, weights),
        out_specs=(rows, rows, weights, weights, weights),
        check_vma=False,
    )
```

```python
import functools

import jax
import jax.numpy as jnp
import numpy as np
from jax import lax
from jax.experimental import pallas as pl
from jax.experimental.pallas import tpu as pltpu
from jax.sharding import PartitionSpec as P

CAP = 3
LEAD = 3
NEAR = LEAD + 2
LAST = NEAR + 1
SUB = 8
LANES = 128
WIDE = SUB * LANES
MESH = pl.DeviceIdType.MESH
F32 = jnp.float32
BF16 = jnp.bfloat16
NT = (((1,), (1,)), ((), ()))
TN = (((0,), (0,)), ((), ()))


def order_matrix(n_ep, per):
    unit = CAP * per
    rows = n_ep * SUB * unit
    out = np.zeros((rows, rows), np.float32)
    for e in range(n_ep):
        for k in range(SUB):
            for kind in range(per):
                for s in range(CAP):
                    out[
                        (e * SUB + k) * unit + kind * CAP + s,
                        ((k * per + kind) * n_ep + e) * CAP + s,
                    ] = 1.0
    return out


def routes(ids, probs, columns):
    tok = ids.shape[1]
    row = lax.broadcasted_iota(jnp.int32, (columns, tok), 0)
    expert = row // CAP
    slot = row - expert * CAP
    match = jnp.zeros((columns, tok), F32)
    weight = jnp.zeros((columns, tok), F32)
    for r in range(ids.shape[0]):
        here = ids[r : r + 1] == expert
        match = jnp.where(here, 1.0, match)
        weight = jnp.where(here, probs[r : r + 1], weight)
    first = lax.broadcasted_iota(jnp.int32, (tok, tok), 0)
    second = lax.broadcasted_iota(jnp.int32, (tok, tok), 1)
    earlier = jnp.where(first < second, 1.0, 0.0).astype(BF16)
    before = jnp.dot(match.astype(BF16), earlier, preferred_element_type=F32)
    live = jnp.where(before == slot.astype(F32), match, 0.0)
    return live, live * weight


def main_kernel(
    n_edp, n_ep,
    tok_ref, cot_ref, probs_ref, ids_ref, wg_ref, wu_ref, wd_ref, ord2_in, ord2t_in, ord1_in, ord1t_in,
    z_out, left_out, back_out, live_out, gg_out,
    ord2_ref, ord2t_ref, ord1_ref, ord1t_ref, left, tok, cot, w, send_a, recv_a, z, acc, send_b, recv_b, send_c, recv_c, own, send_d, recv_d,
    dp, dp_b, dp_s, dp_c, dp_d, dp_r,
    o_sem, l_sem, t_sem, w_sem, z_sem, loc_sem, a_ss, a_rs, e_ss, e_rs, f_ss, f_rs, b_ss, b_rs, c_ss, c_rs, d_ss, d_rs,
    pb_s, pc_ss, pc_rs, pd_ss, pd_rs,
):
    n_ch = z.shape[0]
    hid = wg_ref.shape[1]
    half = n_ep * CAP
    n_q = n_edp // 2
    me_i = lax.axis_index("edp")
    me_j = lax.axis_index("ep")
    q_me = me_i // 2
    core = me_i - q_me * 2
    mate = q_me * 2 + 1 - core

    def w_copy(c, part):
        src = (wg_ref, wu_ref, wd_ref)[part]
        return pltpu.make_async_copy(
            src.at[0, :, pl.ds(pl.multiple_of(c * WIDE, WIDE), WIDE)],
            w.at[c, pl.ds(part * hid, hid), :],
            w_sem.at[c, part],
        )

    def t_copy(c, part):
        src, dst = ((tok_ref, tok), (cot_ref, cot))[part]
        return pltpu.make_async_copy(
            src.at[:, pl.ds(pl.multiple_of(c * WIDE, WIDE), WIDE)], dst.at[c], t_sem.at[c, part]
        )

    o_copies = [
        pltpu.make_async_copy(src, dst, o_sem.at[k])
        for k, (src, dst) in enumerate(
            ((ord2_in, ord2_ref), (ord2t_in, ord2t_ref), (ord1_in, ord1_ref), (ord1t_in, ord1t_ref))
        )
    ]
    for c in range(n_ch):
        t_copy(c, 0).start()
        t_copy(c, 1).start()
        if c < len(o_copies):
            o_copies[c].start()

    barrier = pltpu.get_barrier_semaphore()
    ep_peers = [lax.rem(me_j + o, n_ep) for o in range(1, n_ep)]
    far = [(lax.rem(q_me + o, n_q), o) for o in range(1, n_q)]
    for j in ep_peers:
        pl.semaphore_signal(barrier, inc=1, device_id=(me_i, j), device_id_type=MESH)
    for q, _ in far:
        pl.semaphore_signal(barrier, inc=1, device_id=(q * 2 + core, me_j), device_id_type=MESH)
    pl.semaphore_signal(barrier, inc=1, device_id=(mate, me_j), device_id_type=MESH)

    live, scaled = routes(ids_ref[...], probs_ref[...].astype(F32), half)
    live_out[...] = live.astype(BF16)
    live_t = live.astype(BF16)
    scaled_t = scaled.astype(BF16)
    prob = jnp.sum(scaled, axis=1, keepdims=True)

    for copy in o_copies:
        copy.wait()
    pl.semaphore_wait(barrier, n_ep - 1 + n_q - 1 + 1)

    def remote(src, dst, ss, rs, i, j):
        return pltpu.make_async_remote_copy(
            src_ref=src, dst_ref=dst, send_sem=ss, recv_sem=rs, device_id=(i, j), device_id_type=MESH
        )

    def a_copy(c, j, slot):
        return remote(send_a.at[c, j], recv_a.at[c, slot], a_ss.at[c, j], a_rs.at[c, slot], me_i, j)

    def a_own(c):
        return pltpu.make_async_copy(send_a.at[c, me_j], recv_a.at[c, me_j], loc_sem.at[c])

    def pack(c):
        t_copy(c, 0).wait()
        t_copy(c, 1).wait()
        x = jnp.dot(live_t, tok[c], preferred_element_type=F32)
        y = jnp.dot(scaled_t, cot[c], preferred_element_type=F32)
        parts = []
        for k in range(SUB):
            lanes = slice(k * LANES, (k + 1) * LANES)
            parts += [x[:, lanes], y[:, lanes]]
        mixed = jnp.concatenate(parts, axis=0).astype(BF16)
        packed = jnp.dot(ord2_ref[...], mixed, preferred_element_type=F32)
        send_a[c] = packed.astype(BF16).reshape(send_a.shape[1:])
        for j in ep_peers:
            a_copy(c, j, me_j).start()
        a_own(c).start()
        for part in range(3):
            w_copy(c, part).start()


    def e_copy(c, i, slot, o):
        return remote(z.at[c, me_i], z.at[c, slot], e_ss.at[c, o], e_rs.at[c, o], i, me_j)

    def f_copy(c, slot, o):
        return remote(z.at[c, slot], z.at[c, slot], f_ss.at[c, o], f_rs.at[c, o], mate, me_j)

    def gather(t, _):
        @pl.when(t < n_ch)
        def _():
            pack(t)

        @pl.when((t >= LEAD) & (t < n_ch + LEAD))
        def _():
            c = t - LEAD
            for j in ep_peers:
                a_copy(c, j, j).wait_recv()
            a_own(c).wait()
            mixed = recv_a[c].reshape(ord2_ref.shape[0], LANES)
            rows = jnp.dot(ord2t_ref[...], mixed, preferred_element_type=F32)
            wide = jnp.concatenate(
                [rows[k * 2 * half : (k + 1) * 2 * half] for k in range(SUB)], axis=1
            )
            z[c, me_i] = wide.astype(BF16)
            for q, o in far:
                e_copy(c, q * 2 + core, me_i, o).start()
            e_copy(c, mate, me_i, 0).start()

        @pl.when((t >= NEAR) & (t < n_ch + NEAR))
        def _():
            c = t - NEAR
            for _, o in far:
                from_q = lax.rem(q_me - o + n_q, n_q)
                e_copy(c, from_q * 2 + core, from_q * 2 + core, o).wait_recv()
                f_copy(c, from_q * 2 + core, o).start()

        @pl.when(t >= LAST)
        def _():
            c = t - LAST
            e_copy(c, mate, mate, 0).wait_recv()
            for _, o in far:
                from_q = lax.rem(q_me - o + n_q, n_q)
                f_copy(c, from_q * 2 + 1 - core, o).wait_recv()
            for part in range(3):
                w_copy(c, part).wait()
            rows = z[c].reshape(n_edp * 2 * half, WIDE)
            part = lax.dot_general(w[c], rows, NT, preferred_element_type=F32)

            @pl.when(c == 0)
            def _():
                acc[...] = part

            @pl.when(c > 0)
            def _():
                acc[...] += part

        return 0

    lax.fori_loop(0, n_ch + LAST, gather, 0)

    def z_copy(c):
        return pltpu.make_async_copy(
            z.at[c], z_out.at[:, :, pl.ds(pl.multiple_of(c * WIDE, WIDE), WIDE)], z_sem.at[c]
        )

    def z_start(c, _):
        z_copy(c).start()
        return 0

    lax.fori_loop(0, n_ch, z_start, 0)

    n_rows = n_edp * 2 * half
    a = acc[:hid]
    u = acc[hid : 2 * hid]
    g = pltpu.roll(acc[2 * hid :], n_rows - half, 1)
    lane = lax.broadcasted_iota(jnp.int32, (hid, n_rows), 1)
    is_x = lax.rem(lane // half, 2) == 0
    s = jax.nn.sigmoid(a)
    h = a * s * u
    d_a = jnp.where(is_x, g * u * s * (1.0 + a * (1.0 - s)), 0.0)
    d_u = jnp.where(is_x, g * a * s, 0.0)
    acc[:hid] = d_a
    acc[hid : 2 * hid] = d_u
    acc[2 * hid :] = jnp.where(is_x, h, 0.0)
    dp[...] = jnp.sum(jnp.where(is_x, h * g, 0.0), axis=0, keepdims=True)
    turned = acc[: 2 * hid].T
    both = jnp.concatenate(
        [turned[i * 2 * half : (i * 2 + 1) * half] for i in range(n_edp)], axis=0
    ).astype(BF16)

    def b_copy(c, q):
        return remote(
            send_b.at[c, q * 2 + 1 - core], recv_b.at[c, q], b_ss.at[c, q], b_rs.at[c, q], mate, me_j
        )

    def dpb_copy():
        return remote(dp, dp_b, pb_s.at[0], pb_s.at[1], mate, me_j)

    def c_copy(c, q, o):
        return remote(
            send_c.at[c, o - 1], recv_c.at[c, o - 1], c_ss.at[c, o - 1], c_rs.at[c, o - 1], q * 2 + core, me_j
        )

    def dpc_copy(q, o):
        return remote(dp_s, dp_c.at[o - 1], pc_ss.at[o - 1], pc_rs.at[o - 1], q * 2 + core, me_j)

    def d_copy(c, j, slot):
        return remote(send_d.at[c, j], recv_d.at[c, slot], d_ss.at[c, j], d_rs.at[c, slot], me_i, j)

    def dpd_copy(j, slot):
        return remote(dp_d, dp_r.at[slot], pd_ss.at[j], pd_rs.at[slot], me_i, j)

    dpb_copy().start()

    def give_back(t, _):
        @pl.when(t < n_ch)
        def _():
            c = t
            part = jnp.dot(both, w[c, : 2 * hid, :], preferred_element_type=F32)
            for i in range(n_edp):
                send_b[c, i] = part[i * half : (i + 1) * half].astype(BF16)
            for q in range(n_q):
                b_copy(c, q).start()

        @pl.when((t >= 2) & (t < n_ch + 2))
        def _():
            c = t - 2
            for q in range(n_q):
                b_copy(c, q).wait_recv()
            for q, o in far:
                total = send_b[c, q * 2 + core].astype(F32) + recv_b[c, q].astype(F32)
                send_c[c, o - 1] = total.astype(BF16)
                c_copy(c, q, o).start()
            own[c] = send_b[c, me_i].astype(F32) + recv_b[c, q_me].astype(F32)

            @pl.when(c == 0)
            def _():
                dpb_copy().wait_recv()
                dp_s[...] = dp[...] + dp_b[...]
                for q, o in far:
                    dpc_copy(q, o).start()

        @pl.when(t >= 5)
        def _():
            c = t - 5
            total = own[c]
            for q, o in far:
                c_copy(c, q, o).wait_recv()
                total = total + recv_c[c, o - 1].astype(F32)
            mixed = jnp.concatenate(
                [total[:, k * LANES : (k + 1) * LANES] for k in range(SUB)], axis=0
            ).astype(BF16)
            packed = jnp.dot(ord1_ref[...], mixed, preferred_element_type=F32)
            send_d[c] = packed.astype(BF16).reshape(send_d.shape[1:])
            for j in ep_peers:
                d_copy(c, j, me_j).start()
            recv_d[c, me_j] = send_d[c, me_j]

            @pl.when(c == 0)
            def _():
                whole_dp = dp_s[...]
                for q, o in far:
                    dpc_copy(q, o).wait_recv()
                    whole_dp = whole_dp + dp_c[o - 1]
                dp_d[...] = whole_dp
                dp_r[me_j] = whole_dp
                for j in ep_peers:
                    dpd_copy(j, me_j).start()

        return 0

    lax.fori_loop(0, n_ch + 5, give_back, 0)

    spin = pltpu.roll(acc[2 * hid :], half, 1)
    left[: 2 * hid] = acc[: 2 * hid].astype(BF16)
    left[2 * hid :] = spin.astype(BF16)
    left_copy = pltpu.make_async_copy(left, left_out, l_sem)
    left_copy.start()

    def finish(c, _):
        for j in ep_peers:
            d_copy(c, j, j).wait_recv()
        mixed = recv_d[c].reshape(ord1_ref.shape[0], LANES)
        rows = jnp.dot(ord1t_ref[...], mixed, preferred_element_type=F32)
        wide = jnp.concatenate([rows[k * half : (k + 1) * half] for k in range(SUB)], axis=1)
        back_out[:, pl.ds(pl.multiple_of(c * WIDE, WIDE), WIDE)] = wide.astype(BF16)
        return 0

    lax.fori_loop(0, n_ch, finish, 0)

    for j in ep_peers:
        dpd_copy(j, j).wait_recv()
    at = lax.broadcasted_iota(jnp.int32, (1, n_rows), 1) - (me_i * 2 * half + me_j * CAP)
    row = lax.broadcasted_iota(jnp.int32, (half, 1), 0)
    got = jnp.zeros((half, 1), F32)
    for e in range(n_ep):
        for slot in range(CAP):
            value = jnp.sum(jnp.where(at == slot, dp_r[e], 0.0), axis=1, keepdims=True)
            got = jnp.where(row == e * CAP + slot, value, got)
    got = jnp.where(prob > 0.0, got / jnp.where(prob > 0.0, prob, 1.0), 0.0)
    got = got.astype(BF16).astype(F32)
    value = live * got
    owner = lax.broadcasted_iota(jnp.int32, live.shape, 0) // CAP
    grads = []
    for r in range(ids_ref.shape[0]):
        mine = jnp.where(ids_ref[r : r + 1] == owner, value, 0.0)
        grads.append(jnp.sum(mine, axis=0, keepdims=True))
    gg_out[...] = jnp.concatenate(grads, axis=0).astype(BF16)

    def drain(c, _):
        for j in ep_peers:
            a_copy(c, j, me_j).wait_send()
            d_copy(c, j, me_j).wait_send()
        e_copy(c, mate, me_i, 0).wait_send()
        for q, o in far:
            e_copy(c, q * 2 + core, me_i, o).wait_send()
            f_copy(c, q * 2 + core, o).wait_send()
            c_copy(c, q, o).wait_send()
        for q in range(n_q):
            b_copy(c, q).wait_send()
        z_copy(c).wait()
        return 0

    lax.fori_loop(0, n_ch, drain, 0)
    left_copy.wait()
    dpb_copy().wait_send()
    for q, o in far:
        dpc_copy(q, o).wait_send()
    for j in ep_peers:
        dpd_copy(j, me_j).wait_send()


def exchange(n_edp, n_ep, tokens, cotangent, gate_probs, expert_ids, w_gate, w_up, w_down):
    tok, width = tokens.shape
    hid = w_gate.shape[1]
    half = n_ep * CAP
    n_q = n_edp // 2
    n_far = max(n_q - 1, 1)
    n_ch = width // WIDE
    two = order_matrix(n_ep, 2)
    one = order_matrix(n_ep, 1)
    orders = [jnp.asarray(m, BF16) for m in (two, two.T, one, one.T)]
    vmem = pl.BlockSpec(memory_space=pltpu.VMEM)
    hbm = pl.BlockSpec(memory_space=pl.ANY)
    dma = pltpu.SemaphoreType.DMA
    rows = n_edp * 2 * half
    left = jax.ShapeDtypeStruct((3 * hid, rows), BF16)
    return pl.pallas_call(
        functools.partial(main_kernel, n_edp, n_ep),
        out_shape=(
            jax.ShapeDtypeStruct((n_edp, 2 * half, width), BF16),
            left,
            jax.ShapeDtypeStruct((half, width), BF16),
            jax.ShapeDtypeStruct((half, tok), BF16),
            jax.ShapeDtypeStruct((gate_probs.shape[1], tok), BF16),
        ),
        in_specs=[hbm] * 2 + [vmem] * 2 + [hbm] * 7,
        out_specs=(hbm,) * 2 + (vmem,) * 3,
        scratch_shapes=[
            *[pltpu.VMEM(m.shape, BF16) for m in orders],
            pltpu.VMEM((3 * hid, rows), BF16),
            pltpu.VMEM((n_ch, tok, WIDE), BF16),
            pltpu.VMEM((n_ch, tok, WIDE), BF16),
            pltpu.VMEM((n_ch, 3 * hid, WIDE), BF16),
            pltpu.VMEM((n_ch, n_ep, SUB * 2 * CAP, LANES), BF16),
            pltpu.VMEM((n_ch, n_ep, SUB * 2 * CAP, LANES), BF16),
            pltpu.VMEM((n_ch, n_edp, 2 * half, WIDE), BF16),
            pltpu.VMEM((3 * hid, rows), F32),
            pltpu.VMEM((n_ch, n_edp, half, WIDE), BF16),
            pltpu.VMEM((n_ch, n_q, half, WIDE), BF16),
            pltpu.VMEM((n_ch, n_far, half, WIDE), BF16),
            pltpu.VMEM((n_ch, n_far, half, WIDE), BF16),
            pltpu.VMEM((n_ch, half, WIDE), F32),
            pltpu.VMEM((n_ch, n_ep, SUB * CAP, LANES), BF16),
            pltpu.VMEM((n_ch, n_ep, SUB * CAP, LANES), BF16),
            pltpu.VMEM((1, rows), F32),
            pltpu.VMEM((1, rows), F32),
            pltpu.VMEM((1, rows), F32),
            pltpu.VMEM((n_far, 1, rows), F32),
            pltpu.VMEM((1, rows), F32),
            pltpu.VMEM((n_ep, 1, rows), F32),
            dma((len(orders),)),
            dma,
            dma((n_ch, 2)),
            dma((n_ch, 3)),
            dma((n_ch,)),
            dma((n_ch,)),
            dma((n_ch, n_ep)),
            dma((n_ch, n_ep)),
            dma((n_ch, n_q)),
            dma((n_ch, n_q)),
            dma((n_ch, n_q)),
            dma((n_ch, n_q)),
            dma((n_ch, n_q)),
            dma((n_ch, n_q)),
            dma((n_ch, n_far)),
            dma((n_ch, n_far)),
            dma((n_ch, n_ep)),
            dma((n_ch, n_ep)),
            dma((2,)),
            dma((n_far,)),
            dma((n_far,)),
            dma((n_ep,)),
            dma((n_ep,)),
        ],
        compiler_params=pltpu.CompilerParams(
            collective_id=0, has_side_effects=True, vmem_limit_bytes=60 * 2**20
        ),
    )(tokens, cotangent, gate_probs.T, expert_ids.T, w_gate, w_up, w_down, *orders)


def grads_kernel(z_ref, left_ref, back_ref, live_ref, gg_ref, tg_out, gg_out, wg_out, wu_out, wd_out):
    rows = z_ref[...].reshape(left_ref.shape[1], z_ref.shape[2])
    hid = wg_out.shape[1]
    for part, out in enumerate((wg_out, wu_out, wd_out)):
        out[0] = jnp.dot(
            left_ref[part * hid : (part + 1) * hid], rows, preferred_element_type=F32
        ).astype(BF16)
    tg_out[...] = lax.dot_general(
        live_ref[...], back_ref[...], TN, preferred_element_type=F32
    ).astype(BF16)
    gg_out[...] = gg_ref[...]


def per_device(tokens, cotangent, gate_probs, expert_ids, w_gate, w_up, w_down):
    n_edp = lax.axis_size("edp")
    n_ep = lax.axis_size("ep")
    half = n_ep * CAP
    results = exchange(
        n_edp, n_ep, tokens, cotangent, gate_probs, expert_ids, w_gate, w_up, w_down
    )
    tok, width = tokens.shape
    hid = w_gate.shape[1]
    rows = n_edp * 2 * half
    step = WIDE
    top = gate_probs.shape[1]

    def whole(*shape):
        return pl.BlockSpec(shape, lambda c: (0,) * len(shape))

    w_spec = pl.BlockSpec((1, hid, step), lambda c: (0, 0, c))
    w_shape = jax.ShapeDtypeStruct(w_gate.shape, BF16)
    token_grad, gate_grad, *weight_grads = pl.pallas_call(
        grads_kernel,
        grid=(width // step,),
        out_shape=(
            jax.ShapeDtypeStruct((tok, width), BF16),
            jax.ShapeDtypeStruct((top, tok), BF16),
            w_shape,
            w_shape,
            w_shape,
        ),
        in_specs=[
            pl.BlockSpec((n_edp, 2 * half, step), lambda c: (0, 0, c)),
            whole(3 * hid, rows),
            pl.BlockSpec((half, step), lambda c: (0, c)),
            whole(half, tok),
            whole(top, tok),
        ],
        out_specs=(
            pl.BlockSpec((tok, step), lambda c: (0, c)),
            whole(top, tok),
            w_spec,
            w_spec,
            w_spec,
        ),
        compiler_params=pltpu.CompilerParams(vmem_limit_bytes=63 * 2**20),
    )(*results)
    return (token_grad, gate_grad.T, *weight_grads)


def solution(mesh):
    rows = P(("edp", "ep"), None)
    weights = P("ep", "edp", None)
    return jax.shard_map(
        per_device,
        mesh=mesh,
        in_specs=(rows, rows, rows, rows, weights, weights, weights),
        out_specs=(rows, rows, weights, weights, weights),
        check_vma=False,
    )
```
